512 devices in a mesh: head: 8 (over y), inner: 8 (over z_lo, core), outer: 8 (over x, z_hi).
Axes of the slice: x: 4, y: 8, z: 8 (z_hi: 2, z_lo: 4; z = z_hi * 4 + z_lo), core: 2. Of those that a mesh axis runs over, the one named last changes fastest.
Arguments:
- queries: bfloat16 [16384, 6144], P(('outer', 'inner', 'head')), may hold values from -6 to 6, as said below
- keys: bfloat16 [16384, 1024], P(('outer', 'inner', 'head')), may hold values from -4 to 4, as said below
- values: bfloat16 [16384, 1024], P(('outer', 'inner', 'head')), may hold values from -5 to 5
- order: int32 [128], replicated, may hold values from 0 to 127, as said below
Outputs:
- attended: bfloat16 [16384, 6144], P(('outer', 'inner', 'head'))
The draws below stay inside these ranges and needn't reach their ends.
Inputs may be any that keep to these rules, and one draw needn't show every extreme that they name: Entries of queries stay in the stated range. Entries of keys stay in the stated range. order is a permutation of the 128 blocks; stored blocks 2 r and 2 r + 1 hold sequence blocks c and 127 - c for some c, in either order.
All inputs are finite; a program needn't handle non-finite values.
Results may differ from the reference program's by a relative error of at most 0.0075.
Values may be sent and summed in bfloat16 or wider, within the bound.
No kernel may reach another device: no remote copies, remote signals or barrier semaphores. Data moves between devices by JAX's collectives and lax.ppermute only.
A program may use at most 64 MiB of HBM per device.

```python
import math
import jax
import jax.numpy as jnp
from jax import lax

QUERY_HEADS = 48
KEY_VALUE_HEADS = 8
HEAD_SIZE = 128
CH = 128
SPANS = 128
SEQUENCE_TOKENS = 16384


def shared_parts(key):
    random_basis = jax.random.normal(jax.random.fold_in(key, 11), (SEQUENCE_TOKENS, KEY_VALUE_HEADS, HEAD_SIZE), jnp.float32)
    return random_basis


def draw_keys(key, part):
    random_basis = shared_parts(key)
    keys = jnp.clip(random_basis, -4.0, 4.0)
    return keys.reshape(SEQUENCE_TOKENS, KEY_VALUE_HEADS * HEAD_SIZE).astype(jnp.bfloat16)


def draw_queries(key, part):
    key = jax.random.fold_in(key, 5)
    queries = jnp.clip(jax.random.normal(key, (SEQUENCE_TOKENS, QUERY_HEADS, HEAD_SIZE), jnp.float32), -4.0, 4.0)
    return queries.reshape(SEQUENCE_TOKENS, QUERY_HEADS * HEAD_SIZE).astype(jnp.bfloat16)


def draw_order(key, part):
    key = jax.random.fold_in(key, 7)
    shards = SPANS // 2
    ranks = jax.random.permutation(jax.random.fold_in(key, 1), shards).astype(jnp.int32)
    flips = jax.random.randint(jax.random.fold_in(key, 2), (shards,), 0, 2).astype(jnp.int32)
    first = jnp.where(flips == 1, SPANS - 1 - ranks, ranks).astype(jnp.int32)
    second = (SPANS - 1 - first).astype(jnp.int32)
    return jnp.stack([first, second], axis=1).reshape(SPANS).astype(jnp.int32)


def levels(own_key, dims, pieces, least, high):
    loudness, own = 1.0, jax.random.fold_in(own_key, 6)
    for axis_at, parts in pieces:
        heights = jnp.exp(jax.random.uniform(jax.random.fold_in(own, axis_at), (parts,), jnp.float32, least / len(pieces), high / len(pieces)))
        loudness = loudness * jnp.repeat(heights, dims[axis_at] // parts).reshape([-1 if axis == axis_at else 1 for axis in range(len(dims))])
    return loudness


def centred(key, dims, spread, limit, pieces=(), kind=jnp.bfloat16):
    drawn = jax.random.normal(key, dims, jnp.float32) * spread
    if len(pieces) > 0:
        drawn = levels(key, dims, pieces, -0.22, 0.18) * drawn
    return jnp.clip(drawn, min=-limit, max=limit).astype(kind)


def setup_inputs(seed: int = 0) -> dict:
    arg_keys = jax.random.split(jax.random.key(seed), 5)
    queries = draw_queries(jax.random.fold_in(arg_keys[4], 71), 0)
    keys = draw_keys(jax.random.fold_in(arg_keys[4], 71), 0)
    values = centred(arg_keys[2], (SEQUENCE_TOKENS, KEY_VALUE_HEADS * HEAD_SIZE), 1.0, 5.0, ((0, 512),))
    order = draw_order(jax.random.fold_in(arg_keys[4], 71), 0)
    return {"queries": queries, "keys": keys, "values": values, "order": order}


def reference(queries, keys, values, order):
    query_group = QUERY_HEADS // KEY_VALUE_HEADS
    qblock = math.gcd(SEQUENCE_TOKENS, 512)
    nblock = SEQUENCE_TOKENS // qblock
    scale = 1.0 / math.sqrt(HEAD_SIZE)
    pos = (order[:, None] * CH + jnp.arange(CH, dtype=jnp.int32)[None, :]).reshape(SEQUENCE_TOKENS).astype(jnp.int32)
    query_tensor = queries.reshape(SEQUENCE_TOKENS, KEY_VALUE_HEADS, query_group, HEAD_SIZE)
    key_tensor = keys.reshape(SEQUENCE_TOKENS, KEY_VALUE_HEADS, HEAD_SIZE)
    value_tensor = values.reshape(SEQUENCE_TOKENS, KEY_VALUE_HEADS, HEAD_SIZE)

    def single_head(index):
        qhead = lax.dynamic_index_in_dim(query_tensor, index, 1, keepdims=False)
        khead = lax.dynamic_index_in_dim(key_tensor, index, 1, keepdims=False).astype(jnp.float32)
        vhead = lax.dynamic_index_in_dim(value_tensor, index, 1, keepdims=False).astype(jnp.float32)

        def one_block(block):
            qrows = lax.dynamic_slice_in_dim(qhead, block * qblock, qblock, 0).astype(jnp.float32)
            qpos = lax.dynamic_slice_in_dim(pos, block * qblock, qblock, 0)
            score = jnp.einsum('tgd,sd->tgs', qrows, khead) * scale
            allowed = (pos[None, :] <= qpos[:, None])[:, None, :]
            top = lax.optimization_barrier(jnp.max(jnp.where(allowed, score, -jnp.inf), axis=-1, keepdims=True))
            expo = jnp.where(allowed, jnp.exp(score - top), 0.0)
            total = lax.optimization_barrier(jnp.sum(expo, axis=-1))
            weight = lax.optimization_barrier(expo.astype(jnp.bfloat16))
            summed = jnp.einsum('tgs,sd->tgd', weight.astype(jnp.float32), vhead)
            return (summed / total[:, :, None]).astype(jnp.bfloat16)
        return lax.map(one_block, jnp.arange(nblock, dtype=jnp.int32))
    attention_output = lax.map(single_head, jnp.arange(KEY_VALUE_HEADS, dtype=jnp.int32))
    attention_output = attention_output.reshape(KEY_VALUE_HEADS, SEQUENCE_TOKENS, query_group, HEAD_SIZE)
    return jnp.transpose(attention_output, (1, 0, 2, 3)).reshape(SEQUENCE_TOKENS, QUERY_HEADS * HEAD_SIZE)
```

```python
import functools
import math

import jax
import jax.numpy as jnp
from jax import lax
from jax.experimental import pallas as pl
from jax.experimental.pallas import tpu as pltpu
from jax.sharding import Mesh, PartitionSpec as P

HEADS = 8
GROUP = 6
HD = 128
CH = 128
ROWS = GROUP * CH
NX, NZ = 4, 8
BLOCKS = 2 * NX * NZ
SLICE = CH // 4
C = math.log2(math.e) / math.sqrt(HD)
LOW = -1e30
MASKED = -3e38
GB = 4
OUTR = HD + 16


def positions(order):
    x, zhi, zlo, core = (lax.axis_index(a) for a in ("x", "zhi", "zlo", "core"))
    shard = jnp.arange(NX * NZ, dtype=jnp.int32)
    piece = shard // NZ
    xs = (x + jnp.where(piece == 2, 3, jnp.where(piece == 3, 2, piece))) % NX
    zs = shard % NZ

    def blocks_of(xv, zv, cv):
        r = (xv * NZ + zv) * 2 + cv
        return (r[:, None] * 2 + jnp.arange(2, dtype=jnp.int32)[None, :]).reshape(-1)

    table = jnp.arange(order.shape[0], dtype=jnp.int32)

    def look(ids):
        return jnp.sum(jnp.where(ids[:, None] == table[None, :], order[None, :], 0), axis=1)

    kseq = look(blocks_of(xs, zs, core))
    own = jnp.stack([core, 1 - core])
    qseq = look(blocks_of(jnp.full(2, x), jnp.full(2, zhi * 4 + zlo), own))
    before = kseq[None, :] < qseq[:, None]
    same = kseq[None, :] == qseq[:, None]
    nfull = jnp.sum(before, axis=1)
    rank = jnp.where(before, jnp.cumsum(before, axis=1) - 1, jnp.where(same, nfull[:, None], -1))
    slot = jnp.arange(BLOCKS + 8, dtype=jnp.int32)
    lists = jnp.sum(
        jnp.where(rank[:, :, None] == slot[None, None, :], jnp.arange(BLOCKS)[None, :, None], 0), axis=1
    )
    count = nfull + jnp.sum(same, axis=1)
    return (
        lists.astype(jnp.int32),
        count.astype(jnp.int32),
        (nfull // GB).astype(jnp.int32),
        kseq.astype(jnp.int32),
        qseq.astype(jnp.int32),
    )


def attend(lst, cnt, full, kseq, qseq, q_ref, qo_ref, kv0, kv1, kv2, kv3a, kv3b, own_ref, ownl_ref, send_ref,
           qt, kbuf, vt, acc, top):
    for piece, refs in enumerate(((kv0,), (kv1,), (kv2,), (kv3a, kv3b))):
        for z in range(NZ):
            for w in range(2):
                at = ((piece * NZ + z) * 2 + w) * CH
                for i in range(4):
                    y = 4 * w + i
                    src = refs[0] if len(refs) == 1 else refs[y // 4]
                    yy = y if len(refs) == 1 else y % 4
                    kbuf[at + i * SLICE : at + (i + 1) * SLICE, :] = src[yy, z, :, :HD]
                v = jnp.concatenate(
                    [
                        (refs[0] if len(refs) == 1 else refs[w])[(4 * w + i) if len(refs) == 1 else i, z, :, HD:]
                        for i in range(4)
                    ],
                    axis=0,
                )
                vt[:HD, at : at + CH] = v.T
    vt[HD:, :] = jnp.ones((OUTR - HD, vt.shape[1]), jnp.bfloat16)
    for j in range(4):
        src = q_ref if j < 2 else qo_ref
        for h in range(GROUP):
            t = src[(j % 2) * CH : (j % 2 + 1) * CH, h * HD : (h + 1) * HD].T.astype(jnp.float32) * C
            hi = t.astype(jnp.bfloat16)
            qt[:HD, h * CH : (h + 1) * CH] = hi
            qt[HD:, h * CH : (h + 1) * CH] = (t - hi.astype(jnp.float32)).astype(jnp.bfloat16)
        acc[...] = jnp.zeros_like(acc)
        top[...] = jnp.full_like(top, LOW)

        def step(base, masked):
            ks, vs, ok = [], [], []
            for g in range(GB):
                s = lst[j, base + g]
                r = pl.multiple_of(s * CH, CH)
                ks.append(kbuf[pl.ds(r, CH), :])
                vs.append(vt[:, pl.ds(r, CH)])
                if masked:
                    kpos = jnp.where(base + g < cnt[j], kseq[s], 1 << 20) * CH
                    ok.append(
                        kpos + lax.broadcasted_iota(jnp.int32, (CH, CH), 0)
                        <= qseq[j] * CH + lax.broadcasted_iota(jnp.int32, (CH, CH), 1)
                    )
            k = jnp.concatenate(ks, axis=0)
            k = jnp.concatenate([k, k], axis=1)
            v = jnp.concatenate(vs, axis=1)
            parts = 3
            width = ROWS // parts
            scores = [
                jnp.dot(k, qt[:, c * width : (c + 1) * width], preferred_element_type=jnp.float32)
                for c in range(parts)
            ]
            if masked:
                okay = jnp.concatenate(ok, axis=0)
                okay = jnp.concatenate([okay] * (width // CH), axis=1)
            for c in range(parts):
                s = scores[c]
                if masked:
                    s = jnp.where(okay, s, MASKED)
                cs = slice(c * width, (c + 1) * width)
                old = top[0:1, cs]
                new = jnp.maximum(old, jnp.max(s, axis=0, keepdims=True))
                p = jnp.exp2(s - new).astype(jnp.bfloat16)
                acc[:, cs] = acc[:, cs] * jnp.exp2(old - new) + jnp.dot(v, p, preferred_element_type=jnp.float32)
                top[0:1, cs] = new

        lax.fori_loop(0, full[j], lambda i, c: (step(i * GB, False), c)[1], 0)

        @pl.when(full[j] * GB < cnt[j])
        def _():
            step(full[j] * GB, True)

        total = acc[HD : HD + 1]
        some = total > 0
        safe = jnp.where(some, total, 1.0)
        out = acc[:HD] * jnp.where(some, 1.0 / safe, 0.0)
        level = top[0:1] + jnp.log2(safe)
        if j < 2:
            own_ref[j] = out
            ownl_ref[j] = level
        else:
            send_ref[j - 2, :HD] = out.astype(jnp.bfloat16)
            hi = level.astype(jnp.bfloat16)
            rest = level - hi.astype(jnp.float32)
            mid = rest.astype(jnp.bfloat16)
            low = (rest - mid.astype(jnp.float32)).astype(jnp.bfloat16)
            at = lax.broadcasted_iota(jnp.int32, (OUTR - HD, ROWS), 0)
            rows = jnp.where(at == 0, hi.astype(jnp.float32), jnp.where(at == 1, mid.astype(jnp.float32), low.astype(jnp.float32)))
            send_ref[j - 2, HD:] = rows.astype(jnp.bfloat16)


def merge(own_ref, ownl_ref, got_ref, out_ref):
    for j in range(2):
        tail = got_ref[j, HD:].astype(jnp.float32)
        theirs = tail[0:1] + tail[1:2] + tail[2:3]
        mine = ownl_ref[j]
        high = jnp.maximum(mine, theirs)
        a, b = jnp.exp2(mine - high), jnp.exp2(theirs - high)
        inv = 1.0 / (a + b)
        out = own_ref[j] * (a * inv) + got_ref[j, :HD].astype(jnp.float32) * (b * inv)
        for h in range(GROUP):
            out_ref[j * CH : (j + 1) * CH, h * HD : (h + 1) * HD] = (
                out[:, h * CH : (h + 1) * CH].T.astype(jnp.bfloat16)
            )


def shards(queries, keys, values, order):
    smem = pl.BlockSpec(memory_space=pltpu.SMEM)
    vmem = pl.BlockSpec(memory_space=pltpu.VMEM)
    f32, bf16 = jnp.float32, jnp.bfloat16

    def turn(n, s):
        return [(i, (i + s) % n) for i in range(n)]

    kv = jnp.concatenate([keys.reshape(SLICE, HEADS, HD), values.reshape(SLICE, HEADS, HD)], axis=2)
    kv = jnp.broadcast_to(kv.transpose(1, 0, 2)[:, None], (HEADS, NZ, SLICE, 2 * HD))
    kv = lax.all_to_all(
        kv.reshape(HEADS * NZ, SLICE, 2 * HD), ("head", "zhi", "zlo"), split_axis=0, concat_axis=0, tiled=True
    )
    kv0 = kv.reshape(HEADS, NZ, SLICE, 2 * HD)
    q = lax.all_to_all(queries, "head", split_axis=1, concat_axis=0, tiled=True)
    kv1 = lax.ppermute(kv0, "x", turn(NX, -1))
    kv3 = lax.ppermute(kv0, "x", turn(NX, 1))
    qo = lax.ppermute(q, "core", turn(2, 1))
    kv2a = lax.ppermute(kv1[:4], "x", turn(NX, -1))
    kv2b = lax.ppermute(kv3[4:], "x", turn(NX, 1))
    tables = positions(order)
    own, ownl, send = pl.pallas_call(
        attend,
        out_shape=(
            jax.ShapeDtypeStruct((2, HD, ROWS), f32),
            jax.ShapeDtypeStruct((2, 1, ROWS), f32),
            jax.ShapeDtypeStruct((2, OUTR, ROWS), bf16),
        ),
        in_specs=[smem] * 5 + [vmem] * 7,
        out_specs=(vmem,) * 3,
        scratch_shapes=[
            pltpu.VMEM((2 * HD, ROWS), bf16),
            pltpu.VMEM((BLOCKS * CH, HD), bf16),
            pltpu.VMEM((OUTR, BLOCKS * CH), bf16),
            pltpu.VMEM((OUTR, ROWS), f32),
            pltpu.VMEM((8, ROWS), f32),
        ],
        compiler_params=pltpu.CompilerParams(vmem_limit_bytes=56 << 20),
        name="attend",
    )(*tables, q, qo, kv0, kv1, kv3, kv2a, kv2b)
    got = lax.ppermute(send, "core", turn(2, 1))
    out = pl.pallas_call(
        merge,
        out_shape=jax.ShapeDtypeStruct((2 * CH, ROWS), bf16),
        in_specs=[vmem] * 3,
        out_specs=vmem,
        compiler_params=pltpu.CompilerParams(vmem_limit_bytes=32 << 20),
        name="merge",
    )(own, ownl, got)
    return lax.all_to_all(out, "head", split_axis=0, concat_axis=1, tiled=True)


def solution(mesh):
    split = Mesh(mesh.devices.reshape(HEADS, 4, 2, NX, 2), ("head", "zlo", "core", "x", "zhi"))
    rows = P(("x", "zhi", "zlo", "core", "head"), None)
    return jax.shard_map(
        shards, mesh=split, in_specs=(rows, rows, rows, P()), out_specs=rows, check_vma=False
    )
```

```python
import functools
import math

import jax
import jax.numpy as jnp
from jax import lax
from jax.experimental import pallas as pl
from jax.experimental.pallas import tpu as pltpu
from jax.sharding import Mesh, PartitionSpec as P

HEADS = 8
GROUP = 6
HD = 128
CH = 128
ROWS = GROUP * CH
NX, NZ = 4, 8
SLICE = CH // 4
C = math.log2(math.e) / math.sqrt(HD)
LOW = -1e30
MASKED = -3e38
GB = 4
WIDTH = 256
BEHIND = 0
OUTR = HD + 16
F32, BF16 = jnp.float32, jnp.bfloat16


def spread_queries(q_ref, qt, j, w):
    for h in range(GROUP):
        t = q_ref[w * CH : (w + 1) * CH, h * HD : (h + 1) * HD].T.astype(F32) * C
        hi = t.astype(BF16)
        qt[j, :HD, h * CH : (h + 1) * CH] = hi
        qt[j, HD:, h * CH : (h + 1) * CH] = (t - hi.astype(F32)).astype(BF16)


def fill(piece, at, rows, kbuf, vt):
    for z in range(NZ):
        for w in range(rows // CH):
            to = (at + z * (rows // CH) + w) * CH
            block = piece[4 * w : 4 * w + 4, z].reshape(CH, 2 * HD)
            kbuf[to : to + CH, :] = block[:, :HD]
            vt[:HD, to : to + CH] = block[:, HD:].T
    return at + NZ * (rows // CH)


def attend(stage, sources, *refs):
    first, last = stage == 0, stage == 2
    order, pos = refs[:2]
    refs = refs[2:]
    pieces, refs = refs[: len(sources)], refs[len(sources) :]
    if first:
        q_ref, qo_ref, acc, top, qt = refs[:5]
        refs = refs[5:]
    elif not last:
        qt, acc_in, top_in, acc, top = refs[:5]
        refs = refs[5:]
    else:
        qt, acc_in, top_in, own_ref, ownl_ref, send_ref = refs[:6]
        refs = refs[6:]
        acc, top = acc_in, top_in
        refs, (acc, top) = refs[:-2], refs[-2:]
    kbuf, vt, sa, sb, tabj, tabk, tabv = refs
    x, z, core = pos[0], pos[1], pos[2]

    def stored(xv, zv, cv, w):
        return ((xv * NZ + zv) * 2 + cv) * 2 + w

    blocks = sum(NZ * (rows // CH) for _, _, rows in sources)
    dummy = blocks

    t = jnp.int32(0)
    for j in range(4):
        cv = core if j < 2 else 1 - core
        mine = order[stored(x, z, cv, j % 2)]
        n = t * GB
        start = n
        slot = 0
        for shift, y0, rows in sources:
            xv = (x + shift) % NX
            per = rows // CH

            def scan(i, n, xv=xv, y0=y0, per=per, slot=slot, mine=mine):
                w = i % per + y0 // 4
                tabk[n] = i + slot
                tabv[n] = i + slot
                return n + (order[stored(xv, i // per, core, w)] < mine).astype(jnp.int32)

            n = lax.fori_loop(0, NZ * per, scan, n, unroll=True)
            slot += NZ * per
        steps = (n - start + GB - 1) // GB
        keep = tabk[jnp.maximum(n - 1, 0)]
        for g in range(GB - 1):
            tabk[n + g] = keep
            tabv[n + g] = dummy

        def mark(i, c, j=j):
            tabj[i] = j
            return c

        lax.fori_loop(t, t + steps, mark, 0)
        t = t + steps
    for e in range(3):
        back = jnp.maximum(t - 1, 0)
        tabj[t + e] = jnp.where(t > 0, tabj[back], 0)
        for g in range(GB):
            tabk[(t + e) * GB + g] = jnp.where(t > 0, tabk[back * GB + g], 0)
            tabv[(t + e) * GB + g] = dummy

    at = 0
    for piece, (_, _, rows) in zip(pieces, sources):
        at = fill(piece, at, rows, kbuf, vt)
    vt[HD:, : blocks * CH] = jnp.ones((OUTR - HD, blocks * CH), BF16)
    vt[:, blocks * CH :] = jnp.zeros((OUTR, CH), BF16)

    def scores(i, out):
        k = jnp.concatenate(
            [kbuf[pl.ds(pl.multiple_of(tabk[i * GB + g] * CH, CH), CH), :] for g in range(GB)], axis=0
        )
        out[...] = jnp.dot(jnp.concatenate([k, k], axis=1), qt[tabj[i]], preferred_element_type=F32)

    def gather(i, s_ref):
        j = tabj[i]
        v = jnp.concatenate([vt[:, pl.ds(pl.multiple_of(tabv[i * GB + g] * CH, CH), CH)] for g in range(GB)], axis=1)
        s = s_ref[...]
        old = top[j]
        new = jnp.maximum(old, jnp.max(s, axis=0, keepdims=True))
        p = jnp.exp2(s - new).astype(BF16)
        acc[j] = acc[j] * jnp.exp2(old - new) + jnp.dot(v, p, preferred_element_type=F32)
        top[j] = new

    if first:
        for j in range(4):
            spread_queries(q_ref if j < 2 else qo_ref, qt, j, j % 2)
        below = lax.broadcasted_iota(jnp.int32, (CH, CH), 0) <= lax.broadcasted_iota(jnp.int32, (CH, CH), 1)
        below = jnp.concatenate([below] * GROUP, axis=1)
        for j in range(2):
            r = pl.multiple_of((z * 2 + j) * CH, CH)
            k = kbuf[pl.ds(r, CH), :]
            s = jnp.dot(jnp.concatenate([k, k], axis=1), qt[j], preferred_element_type=F32)
            s = jnp.where(below, s, MASKED)
            high = jnp.max(s, axis=0, keepdims=True)
            p = jnp.exp2(s - high).astype(BF16)
            acc[j] = jnp.dot(vt[:, pl.ds(r, CH)], p, preferred_element_type=F32)
            top[j] = high
        for j in range(2, 4):
            acc[j] = jnp.zeros((OUTR, ROWS), F32)
            top[j] = jnp.full((1, ROWS), LOW, F32)
    else:
        acc[...] = acc_in[...]
        top[...] = top_in[...]

    scores(0, sa)

    def both(i, s_ref, n_ref):
        j, jn = tabj[i], tabj[i + 1]
        k = jnp.concatenate(
            [kbuf[pl.ds(pl.multiple_of(tabk[(i + 1) * GB + g] * CH, CH), CH), :] for g in range(GB)], axis=0
        )
        k = jnp.concatenate([k, k], axis=1)
        v = jnp.concatenate([vt[:, pl.ds(pl.multiple_of(tabv[i * GB + g] * CH, CH), CH)] for g in range(GB)], axis=1)

        def add(cs, old, new, p):
            acc[j, :, cs] = acc[j, :, cs] * jnp.exp2(old - new) + jnp.dot(v, p, preferred_element_type=F32)
            top[j, :, cs] = new

        waiting = []
        for c in range(ROWS // WIDTH):
            cs = slice(c * WIDTH, (c + 1) * WIDTH)
            n_ref[:, cs] = jnp.dot(k, qt[jn, :, cs], preferred_element_type=F32)
            s = s_ref[:, cs]
            old = top[j, :, cs]
            new = jnp.maximum(old, jnp.max(s, axis=0, keepdims=True))
            waiting.append((cs, old, new, jnp.exp2(s - new).astype(BF16)))
            if len(waiting) > BEHIND:
                add(*waiting.pop(0))
        for w in waiting:
            add(*w)

    def pair(i, c):
        both(2 * i, sa, sb)
        both(2 * i + 1, sb, sa)
        return c

    lax.fori_loop(0, (t + 1) // 2, pair, 0)

    if last:
        for j in range(4):
            total = acc[j, HD : HD + 1]
            some = total > 0
            safe = jnp.where(some, total, 1.0)
            out = acc[j, :HD] * jnp.where(some, 1.0 / safe, 0.0)
            level = top[j] + jnp.log2(safe)
            if j < 2:
                own_ref[j] = out
                ownl_ref[j] = level
            else:
                send_ref[j - 2, :HD] = out.astype(BF16)
                hi = level.astype(BF16).astype(F32)
                mid = (level - hi).astype(BF16).astype(F32)
                row = lax.broadcasted_iota(jnp.int32, (OUTR - HD, ROWS), 0)
                tail = jnp.where(row == 0, hi, jnp.where(row == 1, mid, level - hi - mid))
                send_ref[j - 2, HD:] = tail.astype(BF16)


def merge(own_ref, ownl_ref, got_ref, out_ref):
    for j in range(2):
        tail = got_ref[j, HD:].astype(F32)
        theirs = tail[0:1] + tail[1:2] + tail[2:3]
        mine = ownl_ref[j]
        high = jnp.maximum(mine, theirs)
        a, b = jnp.exp2(mine - high), jnp.exp2(theirs - high)
        inv = 1.0 / (a + b)
        out = own_ref[j] * (a * inv) + got_ref[j, :HD].astype(F32) * (b * inv)
        for h in range(GROUP):
            out_ref[j * CH : (j + 1) * CH, h * HD : (h + 1) * HD] = (
                out[:, h * CH : (h + 1) * CH].T.astype(BF16)
            )


VMEM = pl.BlockSpec(memory_space=pltpu.VMEM)
SMEM = pl.BlockSpec(memory_space=pltpu.SMEM)
SOURCES = (((0, 0, 256),), ((1, 0, 256), (3, 0, 256)), ((2, 0, 128), (2, 4, 128)))


def call(stage, order, pos, *arrays):
    sources = SOURCES[stage]
    blocks = sum(NZ * (rows // CH) for _, _, rows in sources)
    state = (jax.ShapeDtypeStruct((4, OUTR, ROWS), F32), jax.ShapeDtypeStruct((4, 1, ROWS), F32))
    scratch = [
        pltpu.VMEM((blocks * CH, HD), BF16),
        pltpu.VMEM((OUTR, (blocks + 1) * CH), BF16),
        pltpu.VMEM((GB * CH, ROWS), F32),
        pltpu.VMEM((GB * CH, ROWS), F32),
        pltpu.SMEM((blocks + 16,), jnp.int32),
        pltpu.SMEM((GB * (blocks + 16),), jnp.int32),
        pltpu.SMEM((GB * (blocks + 16),), jnp.int32),
    ]
    if stage == 0:
        outs = state + (jax.ShapeDtypeStruct((4, 2 * HD, ROWS), BF16),)
    elif stage == 1:
        outs = state
    else:
        outs = (
            jax.ShapeDtypeStruct((2, HD, ROWS), F32),
            jax.ShapeDtypeStruct((2, 1, ROWS), F32),
            jax.ShapeDtypeStruct((2, OUTR, ROWS), BF16),
        )
        scratch += [pltpu.VMEM((4, OUTR, ROWS), F32), pltpu.VMEM((4, 1, ROWS), F32)]
    flops = blocks * 2 * 2 * 2 * HD * CH * ROWS
    return pl.pallas_call(
        functools.partial(attend, stage, sources),
        out_shape=outs,
        in_specs=[SMEM] * 2 + [VMEM] * len(arrays),
        out_specs=(VMEM,) * len(outs),
        scratch_shapes=scratch,
        cost_estimate=pl.CostEstimate(flops=2 * flops, bytes_accessed=blocks * CH * 512, transcendentals=blocks * 2 * CH * ROWS),
        compiler_params=pltpu.CompilerParams(vmem_limit_bytes=20 << 20),
        name=f"attend{stage}",
    )(order, pos, *arrays)


def shards(queries, keys, values, order):
    def turn(n, s):
        return [(i, (i + s) % n) for i in range(n)]

    kv = jnp.concatenate([keys.reshape(SLICE, HEADS, HD), values.reshape(SLICE, HEADS, HD)], axis=2)
    kv = jnp.broadcast_to(kv.transpose(1, 0, 2)[:, None], (HEADS, NZ, SLICE, 2 * HD))
    kv = lax.all_to_all(
        kv.reshape(HEADS * NZ, SLICE, 2 * HD), ("head", "zhi", "zlo"), split_axis=0, concat_axis=0, tiled=True
    )
    kv0 = kv.reshape(HEADS, NZ, SLICE, 2 * HD)
    q = lax.all_to_all(queries, "head", split_axis=1, concat_axis=0, tiled=True)
    kv1 = lax.ppermute(kv0, "x", turn(NX, -1))
    kv3 = lax.ppermute(kv0, "x", turn(NX, 1))
    qo = lax.ppermute(q, "core", turn(2, 1))
    kv2a = lax.ppermute(kv1[:4], "x", turn(NX, -1))
    kv2b = lax.ppermute(kv3[4:], "x", turn(NX, 1))
    pos = jnp.stack(
        [lax.axis_index("x"), lax.axis_index("zhi") * 4 + lax.axis_index("zlo"), lax.axis_index("core")]
    ).astype(jnp.int32)
    acc, top, qt = call(0, order, pos, kv0, q, qo)
    acc, top = call(1, order, pos, kv1, kv3, qt, acc, top)
    own, ownl, send = call(2, order, pos, kv2a, kv2b, qt, acc, top)
    got = lax.ppermute(send, "core", turn(2, 1))
    out = pl.pallas_call(
        merge,
        out_shape=jax.ShapeDtypeStruct((2 * CH, ROWS), BF16),
        in_specs=[VMEM] * 3,
        out_specs=VMEM,
        compiler_params=pltpu.CompilerParams(vmem_limit_bytes=32 << 20),
        name="merge",
    )(own, ownl, got)
    return lax.all_to_all(out, "head", split_axis=0, concat_axis=1, tiled=True)


def solution(mesh):
    split = Mesh(mesh.devices.reshape(HEADS, 4, 2, NX, 2), ("head", "zlo", "core", "x", "zhi"))
    rows = P(("x", "zhi", "zlo", "core", "head"), None)
    return jax.shard_map(
        shards, mesh=split, in_specs=(rows, rows, rows, P()), out_specs=rows, check_vma=False
    )
```

```python
import functools
import math

import jax
import jax.numpy as jnp
from jax import lax
from jax.experimental import pallas as pl
from jax.experimental.pallas import tpu as pltpu
from jax.sharding import Mesh, PartitionSpec as P

HEADS = 8
GROUP = 6
HD = 128
CH = 128
ROWS = GROUP * CH
NX, NZ = 4, 8
SLICE = CH // 4
C = math.log2(math.e) / math.sqrt(HD)
LOW = -1e30
MASKED = -3e38
GB = 4
WIDTH = 256
BEHIND = 0
OUTR = HD + 16
F32, BF16 = jnp.float32, jnp.bfloat16


def spread_queries(q_ref, qt, j, w):
    for h in range(GROUP):
        t = q_ref[w * CH : (w + 1) * CH, h * HD : (h + 1) * HD].T.astype(F32) * C
        hi = t.astype(BF16)
        qt[j, :HD, h * CH : (h + 1) * CH] = hi
        qt[j, HD:, h * CH : (h + 1) * CH] = (t - hi.astype(F32)).astype(BF16)


def fill(piece, at, kbuf, vt):
    for z in range(NZ):
        for w in range(2):
            to = (at + 2 * z + w) * CH
            block = piece[4 * w : 4 * w + 4, z].reshape(CH, 2 * HD)
            kbuf[to : to + CH, :] = block[:, :HD]
            vt[:HD, to : to + CH] = block[:, HD:].T


def attend(stage, sources, *refs):
    first, last = stage == 0, stage == 2
    order, pos = refs[:2]
    refs = refs[2:]
    pieces, refs = refs[: len(sources)], refs[len(sources) :]
    if first:
        q_ref, qo_ref, acc, top, qt = refs[:5]
        refs = refs[5:]
    elif not last:
        qt, acc_in, top_in, acc, top = refs[:5]
        refs = refs[5:]
    else:
        qt, acc_in, top_in, own_ref, ownl_ref, send_ref = refs[:6]
        refs = refs[6:]
        acc, top = acc_in, top_in
        refs, (acc, top) = refs[:-2], refs[-2:]
    kbuf, vt, sa, sb, tabj, tabk, tabv = refs
    x, z, core = pos[0], pos[1], pos[2]

    def stored(xv, zv, cv, w):
        return ((xv * NZ + zv) * 2 + cv) * 2 + w

    blocks = 2 * NZ * len(sources)
    dummy = blocks

    t = jnp.int32(0)
    for j in range(4):
        cv = core if j < 2 else 1 - core
        mine = order[stored(x, z, cv, j % 2)]
        n = t * GB
        start = n
        slot = 0
        for shifts in sources:
            xv = (x + jnp.where(core == 0, *shifts)) % NX

            def scan(i, n, xv=xv, slot=slot, mine=mine):
                tabk[n] = i + slot
                tabv[n] = i + slot
                return n + (order[stored(xv, i // 2, core, i % 2)] < mine).astype(jnp.int32)

            n = lax.fori_loop(0, 2 * NZ, scan, n, unroll=True)
            slot += 2 * NZ
        steps = (n - start + GB - 1) // GB
        keep = tabk[jnp.maximum(n - 1, 0)]
        for g in range(GB - 1):
            tabk[n + g] = keep
            tabv[n + g] = dummy

        def mark(i, c, j=j):
            tabj[i] = j
            return c

        lax.fori_loop(t, t + steps, mark, 0)
        t = t + steps
    for e in range(3):
        back = jnp.maximum(t - 1, 0)
        tabj[t + e] = jnp.where(t > 0, tabj[back], 0)
        for g in range(GB):
            tabk[(t + e) * GB + g] = jnp.where(t > 0, tabk[back * GB + g], 0)
            tabv[(t + e) * GB + g] = dummy

    for at, piece in enumerate(pieces):
        fill(piece, at * 2 * NZ, kbuf, vt)
    vt[HD:, : blocks * CH] = jnp.ones((OUTR - HD, blocks * CH), BF16)
    vt[:, blocks * CH :] = jnp.zeros((OUTR, CH), BF16)

    def scores(i, out):
        k = jnp.concatenate(
            [kbuf[pl.ds(pl.multiple_of(tabk[i * GB + g] * CH, CH), CH), :] for g in range(GB)], axis=0
        )
        out[...] = jnp.dot(jnp.concatenate([k, k], axis=1), qt[tabj[i]], preferred_element_type=F32)

    def gather(i, s_ref):
        j = tabj[i]
        v = jnp.concatenate([vt[:, pl.ds(pl.multiple_of(tabv[i * GB + g] * CH, CH), CH)] for g in range(GB)], axis=1)
        s = s_ref[...]
        old = top[j]
        new = jnp.maximum(old, jnp.max(s, axis=0, keepdims=True))
        p = jnp.exp2(s - new).astype(BF16)
        acc[j] = acc[j] * jnp.exp2(old - new) + jnp.dot(v, p, preferred_element_type=F32)
        top[j] = new

    if first:
        for j in range(4):
            spread_queries(q_ref if j < 2 else qo_ref, qt, j, j % 2)
        below = lax.broadcasted_iota(jnp.int32, (CH, CH), 0) <= lax.broadcasted_iota(jnp.int32, (CH, CH), 1)
        below = jnp.concatenate([below] * GROUP, axis=1)
        for j in range(2):
            r = pl.multiple_of((z * 2 + j) * CH, CH)
            k = kbuf[pl.ds(r, CH), :]
            s = jnp.dot(jnp.concatenate([k, k], axis=1), qt[j], preferred_element_type=F32)
            s = jnp.where(below, s, MASKED)
            high = jnp.max(s, axis=0, keepdims=True)
            p = jnp.exp2(s - high).astype(BF16)
            acc[j] = jnp.dot(vt[:, pl.ds(r, CH)], p, preferred_element_type=F32)
            top[j] = high
        for j in range(2, 4):
            acc[j] = jnp.zeros((OUTR, ROWS), F32)
            top[j] = jnp.full((1, ROWS), LOW, F32)
    else:
        acc[...] = acc_in[...]
        top[...] = top_in[...]

    scores(0, sa)

    def both(i, s_ref, n_ref):
        j, jn = tabj[i], tabj[i + 1]
        k = jnp.concatenate(
            [kbuf[pl.ds(pl.multiple_of(tabk[(i + 1) * GB + g] * CH, CH), CH), :] for g in range(GB)], axis=0
        )
        k = jnp.concatenate([k, k], axis=1)
        v = jnp.concatenate([vt[:, pl.ds(pl.multiple_of(tabv[i * GB + g] * CH, CH), CH)] for g in range(GB)], axis=1)

        def add(cs, old, new, p):
            acc[j, :, cs] = acc[j, :, cs] * jnp.exp2(old - new) + jnp.dot(v, p, preferred_element_type=F32)
            top[j, :, cs] = new

        waiting = []
        for c in range(ROWS // WIDTH):
            cs = slice(c * WIDTH, (c + 1) * WIDTH)
            n_ref[:, cs] = jnp.dot(k, qt[jn, :, cs], preferred_element_type=F32)
            s = s_ref[:, cs]
            old = top[j, :, cs]
            new = jnp.maximum(old, jnp.max(s, axis=0, keepdims=True))
            waiting.append((cs, old, new, jnp.exp2(s - new).astype(BF16)))
            if len(waiting) > BEHIND:
                add(*waiting.pop(0))
        for w in waiting:
            add(*w)

    def pair(i, c):
        both(2 * i, sa, sb)
        both(2 * i + 1, sb, sa)
        return c

    lax.fori_loop(0, (t + 1) // 2, pair, 0)

    if last:
        for j in range(4):
            total = acc[j, HD : HD + 1]
            some = total > 0
            safe = jnp.where(some, total, 1.0)
            out = acc[j, :HD] * jnp.where(some, 1.0 / safe, 0.0)
            level = top[j] + jnp.log2(safe)
            if j < 2:
                own_ref[j] = out
                ownl_ref[j] = level
            else:
                send_ref[j - 2, :HD] = out.astype(BF16)
                hi = level.astype(BF16).astype(F32)
                mid = (level - hi).astype(BF16).astype(F32)
                row = lax.broadcasted_iota(jnp.int32, (OUTR - HD, ROWS), 0)
                tail = jnp.where(row == 0, hi, jnp.where(row == 1, mid, level - hi - mid))
                send_ref[j - 2, HD:] = tail.astype(BF16)


def arrange(k_ref, v_ref, out_ref):
    for h in range(HEADS):
        cols = slice(h * HD, (h + 1) * HD)
        both = jnp.concatenate([k_ref[:, cols], v_ref[:, cols]], axis=1)
        for z in range(NZ):
            out_ref[h, z] = both


def merge(own_ref, ownl_ref, got_ref, out_ref):
    for j in range(2):
        tail = got_ref[j, HD:].astype(F32)
        theirs = tail[0:1] + tail[1:2] + tail[2:3]
        mine = ownl_ref[j]
        high = jnp.maximum(mine, theirs)
        a, b = jnp.exp2(mine - high), jnp.exp2(theirs - high)
        inv = 1.0 / (a + b)
        out = own_ref[j] * (a * inv) + got_ref[j, :HD].astype(F32) * (b * inv)
        for h in range(GROUP):
            out_ref[j * CH : (j + 1) * CH, h * HD : (h + 1) * HD] = (
                out[:, h * CH : (h + 1) * CH].T.astype(BF16)
            )


VMEM = pl.BlockSpec(memory_space=pltpu.VMEM)
SMEM = pl.BlockSpec(memory_space=pltpu.SMEM)
SOURCES = (((0, 0),), ((1, 3), (3, 1)), ((2, 2),))


def call(stage, order, pos, *arrays):
    sources = SOURCES[stage]
    blocks = 2 * NZ * len(sources)
    state = (jax.ShapeDtypeStruct((4, OUTR, ROWS), F32), jax.ShapeDtypeStruct((4, 1, ROWS), F32))
    scratch = [
        pltpu.VMEM((blocks * CH, HD), BF16),
        pltpu.VMEM((OUTR, (blocks + 1) * CH), BF16),
        pltpu.VMEM((GB * CH, ROWS), F32),
        pltpu.VMEM((GB * CH, ROWS), F32),
        pltpu.SMEM((blocks + 16,), jnp.int32),
        pltpu.SMEM((GB * (blocks + 16),), jnp.int32),
        pltpu.SMEM((GB * (blocks + 16),), jnp.int32),
    ]
    if stage == 0:
        outs = state + (jax.ShapeDtypeStruct((4, 2 * HD, ROWS), BF16),)
    elif stage == 1:
        outs = state
    else:
        outs = (
            jax.ShapeDtypeStruct((2, HD, ROWS), F32),
            jax.ShapeDtypeStruct((2, 1, ROWS), F32),
            jax.ShapeDtypeStruct((2, OUTR, ROWS), BF16),
        )
        scratch += [pltpu.VMEM((4, OUTR, ROWS), F32), pltpu.VMEM((4, 1, ROWS), F32)]
    flops = blocks * 2 * 2 * 2 * HD * CH * ROWS
    return pl.pallas_call(
        functools.partial(attend, stage, sources),
        out_shape=outs,
        in_specs=[SMEM] * 2 + [VMEM] * len(arrays),
        out_specs=(VMEM,) * len(outs),
        scratch_shapes=scratch,
        cost_estimate=pl.CostEstimate(flops=2 * flops, bytes_accessed=blocks * CH * 512, transcendentals=blocks * 2 * CH * ROWS),
        compiler_params=pltpu.CompilerParams(vmem_limit_bytes=20 << 20),
        name=f"attend{stage}",
    )(order, pos, *arrays)


def shards(queries, keys, values, order):
    def around(s):
        return [(c * NX + i, c * NX + (i + (s if c else -s)) % NX) for c in range(2) for i in range(NX)]

    kv = pl.pallas_call(
        arrange,
        out_shape=jax.ShapeDtypeStruct((HEADS, NZ, SLICE, 2 * HD), BF16),
        in_specs=[VMEM] * 2,
        out_specs=VMEM,
        name="arrange",
    )(keys, values)
    kv = lax.all_to_all(
        kv.reshape(HEADS * NZ, SLICE, 2 * HD), ("head", "zhi", "zlo"), split_axis=0, concat_axis=0, tiled=True
    )
    kv0 = kv.reshape(HEADS, NZ, SLICE, 2 * HD)
    q = lax.all_to_all(queries, "head", split_axis=1, concat_axis=0, tiled=True)
    kv1 = lax.ppermute(kv0, ("core", "x"), around(1))
    kv3 = lax.ppermute(kv0, ("core", "x"), around(-1))
    qo = lax.ppermute(q, "core", [(0, 1), (1, 0)])
    kv2 = lax.ppermute(kv1, ("core", "x"), around(1))
    pos = jnp.stack(
        [lax.axis_index("x"), lax.axis_index("zhi") * 4 + lax.axis_index("zlo"), lax.axis_index("core")]
    ).astype(jnp.int32)
    acc, top, qt = call(0, order, pos, kv0, q, qo)
    acc, top = call(1, order, pos, kv1, kv3, qt, acc, top)
    own, ownl, send = call(2, order, pos, kv2, qt, acc, top)
    got = lax.ppermute(send, "core", [(0, 1), (1, 0)])
    out = pl.pallas_call(
        merge,
        out_shape=jax.ShapeDtypeStruct((2 * CH, ROWS), BF16),
        in_specs=[VMEM] * 3,
        out_specs=VMEM,
        compiler_params=pltpu.CompilerParams(vmem_limit_bytes=20 << 20),
        name="merge",
    )(own, ownl, got)
    return lax.all_to_all(out, "head", split_axis=0, concat_axis=1, tiled=True)


def solution(mesh):
    split = Mesh(mesh.devices.reshape(HEADS, 4, 2, NX, 2), ("head", "zlo", "core", "x", "zhi"))
    rows = P(("x", "zhi", "zlo", "core", "head"), None)
    return jax.shard_map(
        shards, mesh=split, in_specs=(rows, rows, rows, P()), out_specs=rows, check_vma=False
    )
```

```python
import functools
import math

import jax
import jax.numpy as jnp
from jax import lax
from jax.experimental import pallas as pl
from jax.experimental.pallas import tpu as pltpu
from jax.sharding import Mesh, PartitionSpec as P

HEADS = 8
GROUP = 6
HD = 128
CH = 128
ROWS = GROUP * CH
NX, NZ = 4, 8
SLICE = CH // 4
C = math.log2(math.e) / math.sqrt(HD)
LOW = -1e30
MASKED = -3e38
GB = 4
WIDTH = 768
BEHIND = 0
OUTR = HD + 16
F32, BF16 = jnp.float32, jnp.bfloat16


def spread_queries(q_ref, qt, j, w):
    for h in range(GROUP):
        t = q_ref[w * CH : (w + 1) * CH, h * HD : (h + 1) * HD].T.astype(F32) * C
        hi = t.astype(BF16)
        qt[j, :HD, h * CH : (h + 1) * CH] = hi
        qt[j, HD:, h * CH : (h + 1) * CH] = (t - hi.astype(F32)).astype(BF16)


def fill(piece, at, kbuf, vt):
    for z in range(NZ):
        for w in range(2):
            to = (at + 2 * z + w) * CH
            block = piece[4 * w : 4 * w + 4, z].reshape(CH, 2 * HD)
            kbuf[to : to + CH, :] = block[:, :HD]
            vt[:HD, to : to + CH] = block[:, HD:].T


def attend(stage, sources, *refs):
    first, last = stage == 0, stage == STAGES - 1
    order, pos = refs[:2]
    refs = refs[2:]
    pieces, refs = refs[: len(sources)], refs[len(sources) :]
    if first:
        q_ref, qo_ref, acc, top, qt = refs[:5]
        refs = refs[5:]
    elif not last:
        qt, acc_in, top_in, acc, top = refs[:5]
        refs = refs[5:]
    else:
        qt, acc_in, top_in, own_ref, ownl_ref, send_ref = refs[:6]
        refs = refs[6:]
        acc, top = acc_in, top_in
        refs, (acc, top) = refs[:-2], refs[-2:]
    kbuf, vt, sa, sb, tabj, tabk, tabv = refs
    x, z, core = pos[0], pos[1], pos[2]

    def stored(xv, zv, cv, w):
        return ((xv * NZ + zv) * 2 + cv) * 2 + w

    blocks = 2 * NZ * len(sources)
    dummy = blocks

    t = jnp.int32(0)
    for j in range(4):
        cv = core if j < 2 else 1 - core
        mine = order[stored(x, z, cv, j % 2)]
        n = t * GB
        start = n
        slot = 0
        for shifts in sources:
            xv = (x + jnp.where(core == 0, *shifts)) % NX

            def scan(i, n, xv=xv, slot=slot, mine=mine):
                tabk[n] = i + slot
                tabv[n] = i + slot
                return n + (order[stored(xv, i // 2, core, i % 2)] < mine).astype(jnp.int32)

            n = lax.fori_loop(0, 2 * NZ, scan, n, unroll=True)
            slot += 2 * NZ
        steps = (n - start + GB - 1) // GB
        keep = tabk[jnp.maximum(n - 1, 0)]
        for g in range(GB - 1):
            tabk[n + g] = keep
            tabv[n + g] = dummy

        def mark(i, c, j=j):
            tabj[i] = j
            return c

        lax.fori_loop(t, t + steps, mark, 0)
        t = t + steps
    for e in range(3):
        back = jnp.maximum(t - 1, 0)
        tabj[t + e] = jnp.where(t > 0, tabj[back], 0)
        for g in range(GB):
            tabk[(t + e) * GB + g] = jnp.where(t > 0, tabk[back * GB + g], 0)
            tabv[(t + e) * GB + g] = dummy

    for at, piece in enumerate(pieces):
        fill(piece, at * 2 * NZ, kbuf, vt)
    vt[HD:, : blocks * CH] = jnp.ones((OUTR - HD, blocks * CH), BF16)
    vt[:, blocks * CH :] = jnp.zeros((OUTR, CH), BF16)

    def scores(i, out):
        k = jnp.concatenate(
            [kbuf[pl.ds(pl.multiple_of(tabk[i * GB + g] * CH, CH), CH), :] for g in range(GB)], axis=0
        )
        out[...] = jnp.dot(jnp.concatenate([k, k], axis=1), qt[tabj[i]], preferred_element_type=F32)

    def gather(i, s_ref):
        j = tabj[i]
        v = jnp.concatenate([vt[:, pl.ds(pl.multiple_of(tabv[i * GB + g] * CH, CH), CH)] for g in range(GB)], axis=1)
        s = s_ref[...]
        old = top[j]
        new = jnp.maximum(old, jnp.max(s, axis=0, keepdims=True))
        p = jnp.exp2(s - new).astype(BF16)
        acc[j] = acc[j] * jnp.exp2(old - new) + jnp.dot(v, p, preferred_element_type=F32)
        top[j] = new

    if first:
        for j in range(4):
            spread_queries(q_ref if j < 2 else qo_ref, qt, j, j % 2)
        below = lax.broadcasted_iota(jnp.int32, (CH, CH), 0) <= lax.broadcasted_iota(jnp.int32, (CH, CH), 1)
        below = jnp.concatenate([below] * GROUP, axis=1)
        for j in range(2):
            r = pl.multiple_of((z * 2 + j) * CH, CH)
            k = kbuf[pl.ds(r, CH), :]
            s = jnp.dot(jnp.concatenate([k, k], axis=1), qt[j], preferred_element_type=F32)
            s = jnp.where(below, s, MASKED)
            high = jnp.max(s, axis=0, keepdims=True)
            p = jnp.exp2(s - high).astype(BF16)
            acc[j] = jnp.dot(vt[:, pl.ds(r, CH)], p, preferred_element_type=F32)
            top[j] = high
        for j in range(2, 4):
            acc[j] = jnp.zeros((OUTR, ROWS), F32)
            top[j] = jnp.full((1, ROWS), LOW, F32)
    else:
        acc[...] = acc_in[...]
        top[...] = top_in[...]

    scores(0, sa)

    def both(i, s_ref, n_ref):
        j, jn = tabj[i], tabj[i + 1]
        k = jnp.concatenate(
            [kbuf[pl.ds(pl.multiple_of(tabk[(i + 1) * GB + g] * CH, CH), CH), :] for g in range(GB)], axis=0
        )
        k = jnp.concatenate([k, k], axis=1)
        v = jnp.concatenate([vt[:, pl.ds(pl.multiple_of(tabv[i * GB + g] * CH, CH), CH)] for g in range(GB)], axis=1)

        def add(cs, old, new, p):
            acc[j, :, cs] = acc[j, :, cs] * jnp.exp2(old - new) + jnp.dot(v, p, preferred_element_type=F32)
            top[j, :, cs] = new

        waiting = []
        for c in range(ROWS // WIDTH):
            cs = slice(c * WIDTH, (c + 1) * WIDTH)
            n_ref[:, cs] = jnp.dot(k, qt[jn, :, cs], preferred_element_type=F32)
            s = s_ref[:, cs]
            old = top[j, :, cs]
            new = jnp.maximum(old, jnp.max(s, axis=0, keepdims=True))
            waiting.append((cs, old, new, jnp.exp2(s - new).astype(BF16)))
            if len(waiting) > BEHIND:
                add(*waiting.pop(0))
        for w in waiting:
            add(*w)

    def pair(i, c):
        both(2 * i, sa, sb)
        both(2 * i + 1, sb, sa)
        return c

    pairs = (t + 1) // 2

    def several(i, c):
        for e in range(4):
            pair(4 * i + e, c)
        return c

    many = pairs // 4
    lax.fori_loop(0, many, several, 0)
    lax.fori_loop(many * 4, pairs, pair, 0)

    if last:
        for j in range(4):
            total = acc[j, HD : HD + 1]
            some = total > 0
            safe = jnp.where(some, total, 1.0)
            out = acc[j, :HD] * jnp.where(some, 1.0 / safe, 0.0)
            level = top[j] + jnp.log2(safe)
            if j < 2:
                own_ref[j] = out
                ownl_ref[j] = level
            else:
                send_ref[j - 2, :HD] = out.astype(BF16)
                hi = level.astype(BF16).astype(F32)
                mid = (level - hi).astype(BF16).astype(F32)
                row = lax.broadcasted_iota(jnp.int32, (OUTR - HD, ROWS), 0)
                tail = jnp.where(row == 0, hi, jnp.where(row == 1, mid, level - hi - mid))
                send_ref[j - 2, HD:] = tail.astype(BF16)


def arrange(k_ref, v_ref, out_ref):
    for h in range(HEADS):
        cols = slice(h * HD, (h + 1) * HD)
        both = jnp.concatenate([k_ref[:, cols], v_ref[:, cols]], axis=1)
        for z in range(NZ):
            out_ref[h, z] = both


def merge(own_ref, ownl_ref, got_ref, out_ref):
    for j in range(2):
        tail = got_ref[j, HD:].astype(F32)
        theirs = tail[0:1] + tail[1:2] + tail[2:3]
        mine = ownl_ref[j]
        high = jnp.maximum(mine, theirs)
        a, b = jnp.exp2(mine - high), jnp.exp2(theirs - high)
        inv = 1.0 / (a + b)
        out = own_ref[j] * (a * inv) + got_ref[j, :HD].astype(F32) * (b * inv)
        for h in range(GROUP):
            out_ref[j * CH : (j + 1) * CH, h * HD : (h + 1) * HD] = (
                out[:, h * CH : (h + 1) * CH].T.astype(BF16)
            )


VMEM = pl.BlockSpec(memory_space=pltpu.VMEM)
SMEM = pl.BlockSpec(memory_space=pltpu.SMEM)
SOURCES = (((0, 0), (1, 3), (3, 1)), ((2, 2),))
STAGES = len(SOURCES)


def call(stage, order, pos, *arrays):
    sources = SOURCES[stage]
    blocks = 2 * NZ * len(sources)
    state = (jax.ShapeDtypeStruct((4, OUTR, ROWS), F32), jax.ShapeDtypeStruct((4, 1, ROWS), F32))
    scratch = [
        pltpu.VMEM((blocks * CH, HD), BF16),
        pltpu.VMEM((OUTR, (blocks + 1) * CH), BF16),
        pltpu.VMEM((GB * CH, ROWS), F32),
        pltpu.VMEM((GB * CH, ROWS), F32),
        pltpu.SMEM((blocks + 16,), jnp.int32),
        pltpu.SMEM((GB * (blocks + 16),), jnp.int32),
        pltpu.SMEM((GB * (blocks + 16),), jnp.int32),
    ]
    if stage == 0:
        outs = state + (jax.ShapeDtypeStruct((4, 2 * HD, ROWS), BF16),)
    elif stage < STAGES - 1:
        outs = state
    else:
        outs = (
            jax.ShapeDtypeStruct((2, HD, ROWS), F32),
            jax.ShapeDtypeStruct((2, 1, ROWS), F32),
            jax.ShapeDtypeStruct((2, OUTR, ROWS), BF16),
        )
        scratch += [pltpu.VMEM((4, OUTR, ROWS), F32), pltpu.VMEM((4, 1, ROWS), F32)]
    flops = blocks * 2 * 2 * 2 * HD * CH * ROWS
    return pl.pallas_call(
        functools.partial(attend, stage, sources),
        out_shape=outs,
        in_specs=[SMEM] * 2 + [VMEM] * len(arrays),
        out_specs=(VMEM,) * len(outs),
        scratch_shapes=scratch,
        cost_estimate=pl.CostEstimate(flops=2 * flops, bytes_accessed=blocks * CH * 512, transcendentals=blocks * 2 * CH * ROWS),
        compiler_params=pltpu.CompilerParams(vmem_limit_bytes=20 << 20),
        name=f"attend{stage}",
    )(order, pos, *arrays)


def shards(queries, keys, values, order):
    def around(s):
        return [(c * NX + i, c * NX + (i + (s if c else -s)) % NX) for c in range(2) for i in range(NX)]

    kv = pl.pallas_call(
        arrange,
        out_shape=jax.ShapeDtypeStruct((HEADS, NZ, SLICE, 2 * HD), BF16),
        in_specs=[VMEM] * 2,
        out_specs=VMEM,
        name="arrange",
    )(keys, values)
    kv = lax.all_to_all(
        kv.reshape(HEADS * NZ, SLICE, 2 * HD), ("head", "zhi", "zlo"), split_axis=0, concat_axis=0, tiled=True
    )
    kv0 = kv.reshape(HEADS, NZ, SLICE, 2 * HD)
    q = lax.all_to_all(queries, "head", split_axis=1, concat_axis=0, tiled=True)
    kv1 = lax.ppermute(kv0, ("core", "x"), around(1))
    kv3 = lax.ppermute(kv0, ("core", "x"), around(-1))
    qo = lax.ppermute(q, "core", [(0, 1), (1, 0)])
    kv2 = lax.ppermute(kv1, ("core", "x"), around(1))
    pos = jnp.stack(
        [lax.axis_index("x"), lax.axis_index("zhi") * 4 + lax.axis_index("zlo"), lax.axis_index("core")]
    ).astype(jnp.int32)
    acc, top, qt = call(0, order, pos, kv0, kv1, kv3, q, qo)
    own, ownl, send = call(1, order, pos, kv2, qt, acc, top)
    got = lax.ppermute(send, "core", [(0, 1), (1, 0)])
    out = pl.pallas_call(
        merge,
        out_shape=jax.ShapeDtypeStruct((2 * CH, ROWS), BF16),
        in_specs=[VMEM] * 3,
        out_specs=VMEM,
        compiler_params=pltpu.CompilerParams(vmem_limit_bytes=20 << 20),
        name="merge",
    )(own, ownl, got)
    return lax.all_to_all(out, "head", split_axis=0, concat_axis=1, tiled=True)


def solution(mesh):
    split = Mesh(mesh.devices.reshape(HEADS, 4, 2, NX, 2), ("head", "zlo", "core", "x", "zhi"))
    rows = P(("x", "zhi", "zlo", "core", "head"), None)
    return jax.shard_map(
        shards, mesh=split, in_specs=(rows, rows, rows, P()), out_specs=rows, check_vma=False
    )
```

```python
import functools
import math

import jax
import jax.numpy as jnp
from jax import lax
from jax.experimental import pallas as pl
from jax.experimental.pallas import tpu as pltpu
from jax.sharding import Mesh, PartitionSpec as P

HEADS = 8
GROUP = 6
HD = 128
CH = 128
ROWS = GROUP * CH
NX, NZ = 4, 8
SLICE = CH // 4
C = math.log2(math.e) / math.sqrt(HD)
LOW = -1e30
MASKED = -3e38
GB = 4
WIDTH = 768
BEHIND = 0
OUTR = HD + 16
F32, BF16 = jnp.float32, jnp.bfloat16


def spread_queries(q_ref, qt, j, w):
    for h in range(GROUP):
        t = q_ref[w * CH : (w + 1) * CH, h * HD : (h + 1) * HD].T.astype(F32) * C
        hi = t.astype(BF16)
        qt[j, :HD, h * CH : (h + 1) * CH] = hi
        qt[j, HD:, h * CH : (h + 1) * CH] = (t - hi.astype(F32)).astype(BF16)


def fill(piece, at, kbuf, vt):
    for i in range(2 * NZ):
        w = i % 2
        to = (at + i) * CH
        block = piece[i // 8, 4 * w : 4 * w + 4, i // 2 % 4].reshape(CH, 2 * HD)
        kbuf[to : to + CH, :] = block[:, :HD]
        vt[:HD, to : to + CH] = block[:, HD:].T


def attend(stage, sources, *refs):
    first, last = stage == 0, stage == STAGES - 1
    order, pos = refs[:2]
    refs = refs[2:]
    pieces, refs = refs[: len(sources)], refs[len(sources) :]
    if first:
        q_ref, qo_ref, acc, top, qt = refs[:5]
        refs = refs[5:]
    elif not last:
        qt, acc_in, top_in, acc, top = refs[:5]
        refs = refs[5:]
    else:
        qt, acc_in, top_in, own_ref, ownl_ref, send_ref = refs[:6]
        refs = refs[6:]
        acc, top = acc_in, top_in
        refs, (acc, top) = refs[:-2], refs[-2:]
    kbuf, vt, sa, sb, tabj, tabk, tabv = refs
    x, z, core = pos[0], pos[1], pos[2]

    def stored(xv, zv, cv, w):
        return ((xv * NZ + zv) * 2 + cv) * 2 + w

    blocks = 2 * NZ * len(sources)
    dummy = blocks

    t = jnp.int32(0)
    for j in range(4):
        cv = core if j < 2 else 1 - core
        mine = order[stored(x, z, cv, j % 2)]
        n = t * GB
        start = n
        slot = 0
        for shifts in sources:
            xv = (x + jnp.where(core == 0, *shifts)) % NX

            for i in range(2 * NZ):
                zv = i // 2 % 4 * 2 + (z + i // 8) % 2
                tabk[n] = i + slot
                tabv[n] = i + slot
                n = n + (order[stored(xv, zv, core, i % 2)] < mine).astype(jnp.int32)
            slot += 2 * NZ
        steps = (n - start + GB - 1) // GB
        keep = tabk[jnp.maximum(n - 1, 0)]
        for g in range(GB - 1):
            tabk[n + g] = keep
            tabv[n + g] = dummy

        def mark(i, c, j=j):
            tabj[i] = j
            return c

        lax.fori_loop(t, t + steps, mark, 0)
        t = t + steps
    for e in range(3):
        back = jnp.maximum(t - 1, 0)
        tabj[t + e] = jnp.where(t > 0, tabj[back], 0)
        for g in range(GB):
            tabk[(t + e) * GB + g] = jnp.where(t > 0, tabk[back * GB + g], 0)
            tabv[(t + e) * GB + g] = dummy

    for at, piece in enumerate(pieces):
        fill(piece, at * 2 * NZ, kbuf, vt)
    vt[HD:, : blocks * CH] = jnp.ones((OUTR - HD, blocks * CH), BF16)
    vt[:, blocks * CH :] = jnp.zeros((OUTR, CH), BF16)

    def scores(i, out):
        k = jnp.concatenate(
            [kbuf[pl.ds(pl.multiple_of(tabk[i * GB + g] * CH, CH), CH), :] for g in range(GB)], axis=0
        )
        out[...] = jnp.dot(jnp.concatenate([k, k], axis=1), qt[tabj[i]], preferred_element_type=F32)

    def gather(i, s_ref):
        j = tabj[i]
        v = jnp.concatenate([vt[:, pl.ds(pl.multiple_of(tabv[i * GB + g] * CH, CH), CH)] for g in range(GB)], axis=1)
        s = s_ref[...]
        old = top[j]
        new = jnp.maximum(old, jnp.max(s, axis=0, keepdims=True))
        p = jnp.exp2(s - new).astype(BF16)
        acc[j] = acc[j] * jnp.exp2(old - new) + jnp.dot(v, p, preferred_element_type=F32)
        top[j] = new

    if first:
        for j in range(4):
            spread_queries(q_ref if j < 2 else qo_ref, qt, j, j % 2)
        below = lax.broadcasted_iota(jnp.int32, (CH, CH), 0) <= lax.broadcasted_iota(jnp.int32, (CH, CH), 1)
        below = jnp.concatenate([below] * GROUP, axis=1)
        for j in range(2):
            r = pl.multiple_of((z // 2 * 2 + j) * CH, CH)
            k = kbuf[pl.ds(r, CH), :]
            s = jnp.dot(jnp.concatenate([k, k], axis=1), qt[j], preferred_element_type=F32)
            s = jnp.where(below, s, MASKED)
            high = jnp.max(s, axis=0, keepdims=True)
            p = jnp.exp2(s - high).astype(BF16)
            acc[j] = jnp.dot(vt[:, pl.ds(r, CH)], p, preferred_element_type=F32)
            top[j] = high
        for j in range(2, 4):
            acc[j] = jnp.zeros((OUTR, ROWS), F32)
            top[j] = jnp.full((1, ROWS), LOW, F32)
    else:
        acc[...] = acc_in[...]
        top[...] = top_in[...]

    scores(0, sa)

    def both(i, s_ref, n_ref):
        j, jn = tabj[i], tabj[i + 1]
        k = jnp.concatenate(
            [kbuf[pl.ds(pl.multiple_of(tabk[(i + 1) * GB + g] * CH, CH), CH), :] for g in range(GB)], axis=0
        )
        k = jnp.concatenate([k, k], axis=1)
        v = jnp.concatenate([vt[:, pl.ds(pl.multiple_of(tabv[i * GB + g] * CH, CH), CH)] for g in range(GB)], axis=1)

        def add(cs, old, new, p):
            acc[j, :, cs] = acc[j, :, cs] * jnp.exp2(old - new) + jnp.dot(v, p, preferred_element_type=F32)
            top[j, :, cs] = new

        waiting = []
        for c in range(ROWS // WIDTH):
            cs = slice(c * WIDTH, (c + 1) * WIDTH)
            n_ref[:, cs] = jnp.dot(k, qt[jn, :, cs], preferred_element_type=F32)
            s = s_ref[:, cs]
            old = top[j, :, cs]
            new = jnp.maximum(old, jnp.max(s, axis=0, keepdims=True))
            waiting.append((cs, old, new, jnp.exp2(s - new).astype(BF16)))
            if len(waiting) > BEHIND:
                add(*waiting.pop(0))
        for w in waiting:
            add(*w)

    def pair(i, c):
        both(2 * i, sa, sb)
        both(2 * i + 1, sb, sa)
        return c

    pairs = (t + 1) // 2

    def several(i, c):
        for e in range(4):
            pair(4 * i + e, c)
        return c

    many = pairs // 4
    lax.fori_loop(0, many, several, 0)
    lax.fori_loop(many * 4, pairs, pair, 0)

    if last:
        for j in range(4):
            total = acc[j, HD : HD + 1]
            some = total > 0
            safe = jnp.where(some, total, 1.0)
            out = acc[j, :HD] * jnp.where(some, 1.0 / safe, 0.0)
            level = top[j] + jnp.log2(safe)
            if j < 2:
                own_ref[j] = out
                ownl_ref[j] = level
            else:
                send_ref[j - 2, :HD] = out.astype(BF16)
                hi = level.astype(BF16).astype(F32)
                mid = (level - hi).astype(BF16).astype(F32)
                row = lax.broadcasted_iota(jnp.int32, (OUTR - HD, ROWS), 0)
                tail = jnp.where(row == 0, hi, jnp.where(row == 1, mid, level - hi - mid))
                send_ref[j - 2, HD:] = tail.astype(BF16)


def arrange(k_ref, v_ref, out_ref):
    for h in range(HEADS):
        cols = slice(h * HD, (h + 1) * HD)
        both = jnp.concatenate([k_ref[:, cols], v_ref[:, cols]], axis=1)
        for z in range(NZ // 2):
            out_ref[h, z] = both


def merge(own_ref, ownl_ref, got_ref, out_ref):
    for j in range(2):
        tail = got_ref[j, HD:].astype(F32)
        theirs = tail[0:1] + tail[1:2] + tail[2:3]
        mine = ownl_ref[j]
        high = jnp.maximum(mine, theirs)
        a, b = jnp.exp2(mine - high), jnp.exp2(theirs - high)
        inv = 1.0 / (a + b)
        out = own_ref[j] * (a * inv) + got_ref[j, :HD].astype(F32) * (b * inv)
        for h in range(GROUP):
            out_ref[j * CH : (j + 1) * CH, h * HD : (h + 1) * HD] = (
                out[:, h * CH : (h + 1) * CH].T.astype(BF16)
            )


VMEM = pl.BlockSpec(memory_space=pltpu.VMEM)
SMEM = pl.BlockSpec(memory_space=pltpu.SMEM)
SOURCES = (((0, 0),), ((1, 3), (3, 1)), ((2, 2),))
STAGES = len(SOURCES)


def call(stage, order, pos, *arrays):
    sources = SOURCES[stage]
    blocks = 2 * NZ * len(sources)
    state = (jax.ShapeDtypeStruct((4, OUTR, ROWS), F32), jax.ShapeDtypeStruct((4, 1, ROWS), F32))
    scratch = [
        pltpu.VMEM((blocks * CH, HD), BF16),
        pltpu.VMEM((OUTR, (blocks + 1) * CH), BF16),
        pltpu.VMEM((GB * CH, ROWS), F32),
        pltpu.VMEM((GB * CH, ROWS), F32),
        pltpu.SMEM((blocks + 16,), jnp.int32),
        pltpu.SMEM((GB * (blocks + 16),), jnp.int32),
        pltpu.SMEM((GB * (blocks + 16),), jnp.int32),
    ]
    if stage == 0:
        outs = state + (jax.ShapeDtypeStruct((4, 2 * HD, ROWS), BF16),)
    elif stage < STAGES - 1:
        outs = state
    else:
        outs = (
            jax.ShapeDtypeStruct((2, HD, ROWS), F32),
            jax.ShapeDtypeStruct((2, 1, ROWS), F32),
            jax.ShapeDtypeStruct((2, OUTR, ROWS), BF16),
        )
        scratch += [pltpu.VMEM((4, OUTR, ROWS), F32), pltpu.VMEM((4, 1, ROWS), F32)]
    flops = blocks * 2 * 2 * 2 * HD * CH * ROWS
    return pl.pallas_call(
        functools.partial(attend, stage, sources),
        out_shape=outs,
        in_specs=[SMEM] * 2 + [VMEM] * len(arrays),
        out_specs=(VMEM,) * len(outs),
        scratch_shapes=scratch,
        cost_estimate=pl.CostEstimate(flops=2 * flops, bytes_accessed=blocks * CH * 512, transcendentals=blocks * 2 * CH * ROWS),
        compiler_params=pltpu.CompilerParams(vmem_limit_bytes=20 << 20),
        name=f"attend{stage}",
    )(order, pos, *arrays)


def shards(queries, keys, values, order):
    def around(s):
        return [(c * NX + i, c * NX + (i + (s if c else -s)) % NX) for c in range(2) for i in range(NX)]

    def along_z(z, c):
        return ((z % 4 * 2) + c) * 2 + z // 4

    beside = [(along_z(z, c), along_z((z + (1 if c else -1)) % NZ, c)) for z in range(NZ) for c in range(2)]

    kv = pl.pallas_call(
        arrange,
        out_shape=jax.ShapeDtypeStruct((HEADS, NZ // 2, SLICE, 2 * HD), BF16),
        in_specs=[VMEM] * 2,
        out_specs=VMEM,
        name="arrange",
    )(keys, values)
    kv = lax.all_to_all(
        kv.reshape(HEADS * NZ // 2, SLICE, 2 * HD), ("head", "zhi", "zmid"), split_axis=0, concat_axis=0, tiled=True
    ).reshape(HEADS, NZ // 2, SLICE, 2 * HD)
    kv0 = jnp.stack([kv, lax.ppermute(kv, ("zmid", "zlow", "core", "zhi"), beside)])
    q = lax.all_to_all(queries, "head", split_axis=1, concat_axis=0, tiled=True)
    kv1 = lax.ppermute(kv0, ("core", "x"), around(1))
    kv3 = lax.ppermute(kv0, ("core", "x"), around(-1))
    qo = lax.ppermute(q, "core", [(0, 1), (1, 0)])
    kv2 = lax.ppermute(kv1, ("core", "x"), around(1))
    pos = jnp.stack(
        [lax.axis_index("x"), lax.axis_index("zhi") * 4 + lax.axis_index("zmid") * 2 + lax.axis_index("zlow"), lax.axis_index("core")]
    ).astype(jnp.int32)
    acc, top, qt = call(0, order, pos, kv0, q, qo)
    acc, top = call(1, order, pos, kv1, kv3, qt, acc, top)
    own, ownl, send = call(2, order, pos, kv2, qt, acc, top)
    got = lax.ppermute(send, "core", [(0, 1), (1, 0)])
    out = pl.pallas_call(
        merge,
        out_shape=jax.ShapeDtypeStruct((2 * CH, ROWS), BF16),
        in_specs=[VMEM] * 3,
        out_specs=VMEM,
        compiler_params=pltpu.CompilerParams(vmem_limit_bytes=20 << 20),
        name="merge",
    )(own, ownl, got)
    return lax.all_to_all(out, "head", split_axis=0, concat_axis=1, tiled=True)


def solution(mesh):
    split = Mesh(mesh.devices.reshape(HEADS, 2, 2, 2, NX, 2), ("head", "zmid", "zlow", "core", "x", "zhi"))
    rows = P(("x", "zhi", "zmid", "zlow", "core", "head"), None)
    return jax.shard_map(
        shards, mesh=split, in_specs=(rows, rows, rows, P()), out_specs=rows, check_vma=False
    )
```

```python
import functools
import math

import jax
import jax.numpy as jnp
from jax import lax
from jax.experimental import pallas as pl
from jax.experimental.pallas import tpu as pltpu
from jax.sharding import Mesh, PartitionSpec as P

HEADS = 8
GROUP = 6
HD = 128
CH = 128
ROWS = GROUP * CH
NX, NZ = 4, 8
SLICE = CH // 4
C = math.log2(math.e) / math.sqrt(HD)
LOW = -1e30
MASKED = -3e38
GB = 4
WIDTH = 768
BEHIND = 0
OUTR = HD + 16
F32, BF16 = jnp.float32, jnp.bfloat16


def spread_queries(q_ref, qt, j, w):
    for h in range(GROUP):
        t = q_ref[w * CH : (w + 1) * CH, h * HD : (h + 1) * HD].T.astype(F32) * C
        hi = t.astype(BF16)
        qt[j, :HD, h * CH : (h + 1) * CH] = hi
        qt[j, HD:, h * CH : (h + 1) * CH] = (t - hi.astype(F32)).astype(BF16)


def fill(piece, at, kbuf, vt):
    for i in range(2 * NZ):
        w = i % 2
        to = (at + i) * CH
        block = piece[i // 8, 4 * w : 4 * w + 4, i // 2 % 4].reshape(CH, 2 * HD)
        kbuf[to : to + CH, :] = block[:, :HD]
        vt[:HD, to : to + CH] = block[:, HD:].T


def attend(stage, sources, *refs):
    first, last = stage == 0, stage == STAGES - 1
    order, pos = refs[:2]
    refs = refs[2:]
    pieces, refs = refs[: len(sources)], refs[len(sources) :]
    if first:
        q_ref, qo_ref, acc, top, qt = refs[:5]
        refs = refs[5:]
    elif not last:
        qt, acc_in, top_in, acc, top = refs[:5]
        refs = refs[5:]
    else:
        qt, acc_in, top_in, own_ref, ownl_ref, send_ref = refs[:6]
        refs = refs[6:]
        acc, top = acc_in, top_in
        refs, (acc, top) = refs[:-2], refs[-2:]
    kbuf, vt, sa, sb, tabj, tabk, tabv = refs
    x, z, core = pos[0], pos[1], pos[2]

    def stored(xv, zv, cv, w):
        return ((xv * NZ + zv) * 2 + cv) * 2 + w

    blocks = 2 * NZ * len(sources)
    dummy = blocks

    t = jnp.int32(0)
    for j in range(4):
        cv = core if j < 2 else 1 - core
        mine = order[stored(x, z, cv, j % 2)]
        n = t * GB
        start = n
        slot = 0
        for shifts in sources:
            xv = (x + jnp.where(core == 0, *shifts)) % NX

            for i in range(2 * NZ):
                zv = i // 2 % 4 * 2 + (z + i // 8) % 2
                tabk[n] = i + slot
                tabv[n] = i + slot
                n = n + (order[stored(xv, zv, core, i % 2)] < mine).astype(jnp.int32)
            slot += 2 * NZ
        steps = (n - start + GB - 1) // GB
        keep = tabk[jnp.maximum(n - 1, 0)]
        for g in range(GB - 1):
            tabk[n + g] = keep
            tabv[n + g] = dummy

        def mark(i, c, j=j):
            tabj[i] = j
            return c

        lax.fori_loop(t, t + steps, mark, 0)
        t = t + steps
    for e in range(3):
        back = jnp.maximum(t - 1, 0)
        tabj[t + e] = jnp.where(t > 0, tabj[back], 0)
        for g in range(GB):
            tabk[(t + e) * GB + g] = jnp.where(t > 0, tabk[back * GB + g], 0)
            tabv[(t + e) * GB + g] = dummy

    for at, piece in enumerate(pieces):
        fill(piece, at * 2 * NZ, kbuf, vt)
    vt[HD:, : blocks * CH] = jnp.ones((OUTR - HD, blocks * CH), BF16)
    vt[:, blocks * CH :] = jnp.zeros((OUTR, CH), BF16)

    def scores(i, out):
        k = jnp.concatenate(
            [kbuf[pl.ds(pl.multiple_of(tabk[i * GB + g] * CH, CH), CH), :] for g in range(GB)], axis=0
        )
        out[...] = jnp.dot(jnp.concatenate([k, k], axis=1), qt[tabj[i]], preferred_element_type=F32)

    def gather(i, s_ref):
        j = tabj[i]
        v = jnp.concatenate([vt[:, pl.ds(pl.multiple_of(tabv[i * GB + g] * CH, CH), CH)] for g in range(GB)], axis=1)
        s = s_ref[...]
        old = top[j]
        new = jnp.maximum(old, jnp.max(s, axis=0, keepdims=True))
        p = jnp.exp2(s - new).astype(BF16)
        acc[j] = acc[j] * jnp.exp2(old - new) + jnp.dot(v, p, preferred_element_type=F32)
        top[j] = new

    if first:
        for j in range(4):
            spread_queries(q_ref if j < 2 else qo_ref, qt, j, j % 2)
        below = lax.broadcasted_iota(jnp.int32, (CH, CH), 0) <= lax.broadcasted_iota(jnp.int32, (CH, CH), 1)
        below = jnp.concatenate([below] * GROUP, axis=1)
        for j in range(2):
            r = pl.multiple_of((z // 2 * 2 + j) * CH, CH)
            k = kbuf[pl.ds(r, CH), :]
            s = jnp.dot(jnp.concatenate([k, k], axis=1), qt[j], preferred_element_type=F32)
            s = jnp.where(below, s, MASKED)
            high = jnp.max(s, axis=0, keepdims=True)
            p = jnp.exp2(s - high).astype(BF16)
            acc[j] = jnp.dot(vt[:, pl.ds(r, CH)], p, preferred_element_type=F32)
            top[j] = high
        for j in range(2, 4):
            acc[j] = jnp.zeros((OUTR, ROWS), F32)
            top[j] = jnp.full((1, ROWS), LOW, F32)
    else:
        acc[...] = acc_in[...]
        top[...] = top_in[...]

    scores(0, sa)

    def both(i, s_ref, n_ref):
        j, jn = tabj[i], tabj[i + 1]
        k = jnp.concatenate(
            [kbuf[pl.ds(pl.multiple_of(tabk[(i + 1) * GB + g] * CH, CH), CH), :] for g in range(GB)], axis=0
        )
        k = jnp.concatenate([k, k], axis=1)
        v = jnp.concatenate([vt[:, pl.ds(pl.multiple_of(tabv[i * GB + g] * CH, CH), CH)] for g in range(GB)], axis=1)

        def add(cs, old, new, p):
            acc[j, :, cs] = acc[j, :, cs] * jnp.exp2(old - new) + jnp.dot(v, p, preferred_element_type=F32)
            top[j, :, cs] = new

        waiting = []
        for c in range(ROWS // WIDTH):
            cs = slice(c * WIDTH, (c + 1) * WIDTH)
            n_ref[:, cs] = jnp.dot(k, qt[jn, :, cs], preferred_element_type=F32)
            s = s_ref[:, cs]
            old = top[j, :, cs]
            new = jnp.maximum(old, jnp.max(s, axis=0, keepdims=True))
            waiting.append((cs, old, new, jnp.exp2(s - new).astype(BF16)))
            if len(waiting) > BEHIND:
                add(*waiting.pop(0))
        for w in waiting:
            add(*w)

    def pair(i, c):
        both(2 * i, sa, sb)
        both(2 * i + 1, sb, sa)
        return c

    pairs = (t + 1) // 2

    def several(i, c):
        for e in range(4):
            pair(4 * i + e, c)
        return c

    many = pairs // 4
    lax.fori_loop(0, many, several, 0)
    lax.fori_loop(many * 4, pairs, pair, 0)

    if last:
        for j in range(4):
            total = acc[j, HD : HD + 1]
            some = total > 0
            safe = jnp.where(some, total, 1.0)
            out = acc[j, :HD] * jnp.where(some, 1.0 / safe, 0.0)
            level = top[j] + jnp.log2(safe)
            if j < 2:
                own_ref[j] = out
                ownl_ref[j] = level
            else:
                send_ref[j - 2, :HD] = out.astype(BF16)
                hi = level.astype(BF16).astype(F32)
                mid = (level - hi).astype(BF16).astype(F32)
                row = lax.broadcasted_iota(jnp.int32, (OUTR - HD, ROWS), 0)
                tail = jnp.where(row == 0, hi, jnp.where(row == 1, mid, level - hi - mid))
                send_ref[j - 2, HD:] = tail.astype(BF16)


def arrange(k_ref, v_ref, q_ref, out_ref, qout_ref):
    for h in range(HEADS):
        qout_ref[h] = q_ref[:, h * ROWS : (h + 1) * ROWS]
    for h in range(HEADS):
        cols = slice(h * HD, (h + 1) * HD)
        both = jnp.concatenate([k_ref[:, cols], v_ref[:, cols]], axis=1)
        for z in range(NZ // 2):
            out_ref[h, z] = both


def merge(own_ref, ownl_ref, got_ref, out_ref):
    for j in range(2):
        tail = got_ref[j, HD:].astype(F32)
        theirs = tail[0:1] + tail[1:2] + tail[2:3]
        mine = ownl_ref[j]
        high = jnp.maximum(mine, theirs)
        a, b = jnp.exp2(mine - high), jnp.exp2(theirs - high)
        inv = 1.0 / (a + b)
        out = own_ref[j] * (a * inv) + got_ref[j, :HD].astype(F32) * (b * inv)
        for h in range(GROUP):
            out_ref[j * CH : (j + 1) * CH, h * HD : (h + 1) * HD] = (
                out[:, h * CH : (h + 1) * CH].T.astype(BF16)
            )


VMEM = pl.BlockSpec(memory_space=pltpu.VMEM)
SMEM = pl.BlockSpec(memory_space=pltpu.SMEM)
SOURCES = (((0, 0),), ((1, 3), (3, 1)), ((2, 2),))
STAGES = len(SOURCES)


def call(stage, order, pos, *arrays):
    sources = SOURCES[stage]
    blocks = 2 * NZ * len(sources)
    state = (jax.ShapeDtypeStruct((4, OUTR, ROWS), F32), jax.ShapeDtypeStruct((4, 1, ROWS), F32))
    scratch = [
        pltpu.VMEM((blocks * CH, HD), BF16),
        pltpu.VMEM((OUTR, (blocks + 1) * CH), BF16),
        pltpu.VMEM((GB * CH, ROWS), F32),
        pltpu.VMEM((GB * CH, ROWS), F32),
        pltpu.SMEM((blocks + 16,), jnp.int32),
        pltpu.SMEM((GB * (blocks + 16),), jnp.int32),
        pltpu.SMEM((GB * (blocks + 16),), jnp.int32),
    ]
    if stage == 0:
        outs = state + (jax.ShapeDtypeStruct((4, 2 * HD, ROWS), BF16),)
    elif stage < STAGES - 1:
        outs = state
    else:
        outs = (
            jax.ShapeDtypeStruct((2, HD, ROWS), F32),
            jax.ShapeDtypeStruct((2, 1, ROWS), F32),
            jax.ShapeDtypeStruct((2, OUTR, ROWS), BF16),
        )
        scratch += [pltpu.VMEM((4, OUTR, ROWS), F32), pltpu.VMEM((4, 1, ROWS), F32)]
    flops = blocks * 2 * 2 * 2 * HD * CH * ROWS
    return pl.pallas_call(
        functools.partial(attend, stage, sources),
        out_shape=outs,
        in_specs=[SMEM] * 2 + [VMEM] * len(arrays),
        out_specs=(VMEM,) * len(outs),
        scratch_shapes=scratch,
        cost_estimate=pl.CostEstimate(flops=2 * flops, bytes_accessed=blocks * CH * 512, transcendentals=blocks * 2 * CH * ROWS),
        compiler_params=pltpu.CompilerParams(vmem_limit_bytes=20 << 20),
        name=f"attend{stage}",
    )(order, pos, *arrays)


def shards(queries, keys, values, order):
    def around(s):
        return [(c * NX + i, c * NX + (i + (s if c else -s)) % NX) for c in range(2) for i in range(NX)]

    def along_z(z, c):
        return ((z % 4 * 2) + c) * 2 + z // 4

    beside = [(along_z(z, c), along_z((z + (1 if c else -1)) % NZ, c)) for z in range(NZ) for c in range(2)]

    kv, q = pl.pallas_call(
        arrange,
        out_shape=(
            jax.ShapeDtypeStruct((HEADS, NZ // 2, SLICE, 2 * HD), BF16),
            jax.ShapeDtypeStruct((HEADS, SLICE, ROWS), BF16),
        ),
        in_specs=[VMEM] * 3,
        out_specs=(VMEM,) * 2,
        name="arrange",
    )(keys, values, queries)
    kv = lax.all_to_all(
        kv.reshape(HEADS * NZ // 2, SLICE, 2 * HD), ("head", "zhi", "zmid"), split_axis=0, concat_axis=0, tiled=True
    ).reshape(HEADS, NZ // 2, SLICE, 2 * HD)
    kv0 = jnp.stack([kv, lax.ppermute(kv, ("zmid", "zlow", "core", "zhi"), beside)])
    q = lax.all_to_all(q, "head", split_axis=0, concat_axis=0, tiled=True).reshape(2 * CH, ROWS)
    kv1 = lax.ppermute(kv0, ("core", "x"), around(1))
    kv3 = lax.ppermute(kv0, ("core", "x"), around(-1))
    qo = lax.ppermute(q, "core", [(0, 1), (1, 0)])
    pos = jnp.stack(
        [lax.axis_index("x"), lax.axis_index("zhi") * 4 + lax.axis_index("zmid") * 2 + lax.axis_index("zlow"), lax.axis_index("core")]
    ).astype(jnp.int32)
    acc, top, qt = call(0, order, pos, kv0, q, qo)
    kv1, kv3, top = lax.optimization_barrier((kv1, kv3, top))
    kv2 = lax.ppermute(kv1, ("core", "x"), around(1))
    acc, top = call(1, order, pos, kv1, kv3, qt, acc, top)
    own, ownl, send = call(2, order, pos, kv2, qt, acc, top)
    got = lax.ppermute(send, "core", [(0, 1), (1, 0)])
    out = pl.pallas_call(
        merge,
        out_shape=jax.ShapeDtypeStruct((2 * CH, ROWS), BF16),
        in_specs=[VMEM] * 3,
        out_specs=VMEM,
        compiler_params=pltpu.CompilerParams(vmem_limit_bytes=20 << 20),
        name="merge",
    )(own, ownl, got)
    return lax.all_to_all(out, "head", split_axis=0, concat_axis=1, tiled=True)


def solution(mesh):
    split = Mesh(mesh.devices.reshape(HEADS, 2, 2, 2, NX, 2), ("head", "zmid", "zlow", "core", "x", "zhi"))
    rows = P(("x", "zhi", "zmid", "zlow", "core", "head"), None)
    return jax.shard_map(
        shards, mesh=split, in_specs=(rows, rows, rows, P()), out_specs=rows, check_vma=False
    )
```

```python
import functools
import math

import jax
import jax.numpy as jnp
from jax import lax
from jax.experimental import pallas as pl
from jax.experimental.pallas import tpu as pltpu
from jax.sharding import Mesh, PartitionSpec as P

HEADS = 8
GROUP = 6
HD = 128
CH = 128
ROWS = GROUP * CH
NX, NZ = 4, 8
SLICE = CH // 4
C = math.log2(math.e) / math.sqrt(HD)
LOW = -1e30
MASKED = -3e38
GB = 4
WIDTH = 768
BEHIND = 0
OUTR = HD + 16
F32, BF16 = jnp.float32, jnp.bfloat16


def spread_queries(q_ref, qt, j, w):
    for h in range(GROUP):
        t = q_ref[w * CH : (w + 1) * CH, h * HD : (h + 1) * HD].T.astype(F32) * C
        hi = t.astype(BF16)
        qt[j, :HD, h * CH : (h + 1) * CH] = hi
        qt[j, HD:, h * CH : (h + 1) * CH] = (t - hi.astype(F32)).astype(BF16)


def fill(piece, at, kbuf, vt):
    for i in range(2 * NZ):
        w = i % 2
        to = (at + i) * CH
        block = piece[i // 8, 4 * w : 4 * w + 4, i // 2 % 4].reshape(CH, 2 * HD)
        kbuf[to : to + CH, :] = block[:, :HD]
        vt[:HD, to : to + CH] = block[:, HD:].T


def attend(stage, sources, *refs):
    first, last = stage == 0, stage == STAGES - 1
    order, pos = refs[:2]
    refs = refs[2:]
    pieces, refs = refs[: len(sources)], refs[len(sources) :]
    if first:
        q_ref, qo_ref, acc, top, qt = refs[:5]
        refs = refs[5:]
    elif not last:
        qt, acc_in, top_in, acc, top = refs[:5]
        refs = refs[5:]
    else:
        qt, acc_in, top_in, own_ref, ownl_ref, send_ref = refs[:6]
        refs = refs[6:]
        acc, top = acc_in, top_in
        refs, (acc, top) = refs[:-2], refs[-2:]
    kbuf, vt, sa, sb, tabj, tabk, tabv = refs
    x, z, core = pos[0], pos[1], pos[2]

    def stored(xv, zv, cv, w):
        return ((xv * NZ + zv) * 2 + cv) * 2 + w

    blocks = 2 * NZ * len(sources)
    dummy = blocks

    t = jnp.int32(0)
    for j in range(4):
        cv = core if j < 2 else 1 - core
        mine = order[stored(x, z, cv, j % 2)]
        n = t * GB
        start = n
        slot = 0
        for shifts in sources:
            xv = (x + jnp.where(core == 0, *shifts)) % NX

            for i in range(2 * NZ):
                zv = i // 2 % 4 * 2 + (z + i // 8) % 2
                tabk[n] = i + slot
                tabv[n] = i + slot
                n = n + (order[stored(xv, zv, core, i % 2)] < mine).astype(jnp.int32)
            slot += 2 * NZ
        steps = (n - start + GB - 1) // GB
        keep = tabk[jnp.maximum(n - 1, 0)]
        for g in range(GB - 1):
            tabk[n + g] = keep
            tabv[n + g] = dummy

        def mark(i, c, j=j):
            tabj[i] = j
            return c

        lax.fori_loop(t, t + steps, mark, 0)
        t = t + steps
    for e in range(3):
        back = jnp.maximum(t - 1, 0)
        tabj[t + e] = jnp.where(t > 0, tabj[back], 0)
        for g in range(GB):
            tabk[(t + e) * GB + g] = jnp.where(t > 0, tabk[back * GB + g], 0)
            tabv[(t + e) * GB + g] = dummy

    for at, piece in enumerate(pieces):
        fill(piece, at * 2 * NZ, kbuf, vt)
    vt[HD:, : blocks * CH] = jnp.ones((OUTR - HD, blocks * CH), BF16)
    vt[:, blocks * CH :] = jnp.zeros((OUTR, CH), BF16)

    def scores(i, out):
        k = jnp.concatenate(
            [kbuf[pl.ds(pl.multiple_of(tabk[i * GB + g] * CH, CH), CH), :] for g in range(GB)], axis=0
        )
        out[...] = jnp.dot(jnp.concatenate([k, k], axis=1), qt[tabj[i]], preferred_element_type=F32)

    def gather(i, s_ref):
        j = tabj[i]
        v = jnp.concatenate([vt[:, pl.ds(pl.multiple_of(tabv[i * GB + g] * CH, CH), CH)] for g in range(GB)], axis=1)
        s = s_ref[...]
        old = top[j]
        new = jnp.maximum(old, jnp.max(s, axis=0, keepdims=True))
        p = jnp.exp2(s - new).astype(BF16)
        acc[j] = acc[j] * jnp.exp2(old - new) + jnp.dot(v, p, preferred_element_type=F32)
        top[j] = new

    if first:
        for j in range(4):
            spread_queries(q_ref if j < 2 else qo_ref, qt, j, j % 2)
        below = lax.broadcasted_iota(jnp.int32, (CH, CH), 0) <= lax.broadcasted_iota(jnp.int32, (CH, CH), 1)
        below = jnp.concatenate([below] * GROUP, axis=1)
        for j in range(2):
            r = pl.multiple_of((z // 2 * 2 + j) * CH, CH)
            k = kbuf[pl.ds(r, CH), :]
            s = jnp.dot(jnp.concatenate([k, k], axis=1), qt[j], preferred_element_type=F32)
            s = jnp.where(below, s, MASKED)
            high = jnp.max(s, axis=0, keepdims=True)
            p = jnp.exp2(s - high).astype(BF16)
            acc[j] = jnp.dot(vt[:, pl.ds(r, CH)], p, preferred_element_type=F32)
            top[j] = high
        for j in range(2, 4):
            acc[j] = jnp.zeros((OUTR, ROWS), F32)
            top[j] = jnp.full((1, ROWS), LOW, F32)
    else:
        acc[...] = acc_in[...]
        top[...] = top_in[...]

    scores(0, sa)

    def both(i, s_ref, n_ref):
        j, jn = tabj[i], tabj[i + 1]
        k = jnp.concatenate(
            [kbuf[pl.ds(pl.multiple_of(tabk[(i + 1) * GB + g] * CH, CH), CH), :] for g in range(GB)], axis=0
        )
        k = jnp.concatenate([k, k], axis=1)
        v = jnp.concatenate([vt[:, pl.ds(pl.multiple_of(tabv[i * GB + g] * CH, CH), CH)] for g in range(GB)], axis=1)

        def add(cs, old, new, p):
            acc[j, :, cs] = acc[j, :, cs] * jnp.exp2(old - new) + jnp.dot(v, p, preferred_element_type=F32)
            top[j, :, cs] = new

        waiting = []
        for c in range(ROWS // WIDTH):
            cs = slice(c * WIDTH, (c + 1) * WIDTH)
            n_ref[:, cs] = jnp.dot(k, qt[jn, :, cs], preferred_element_type=F32)
            s = s_ref[:, cs]
            old = top[j, :, cs]
            new = jnp.maximum(old, jnp.max(s, axis=0, keepdims=True))
            waiting.append((cs, old, new, jnp.exp2(s - new).astype(BF16)))
            if len(waiting) > BEHIND:
                add(*waiting.pop(0))
        for w in waiting:
            add(*w)

    def pair(i, c):
        both(2 * i, sa, sb)
        both(2 * i + 1, sb, sa)
        return c

    pairs = (t + 1) // 2

    def several(i, c):
        for e in range(4):
            pair(4 * i + e, c)
        return c

    many = pairs // 4
    lax.fori_loop(0, many, several, 0)
    lax.fori_loop(many * 4, pairs, pair, 0)

    if last:
        for j in range(4):
            total = acc[j, HD : HD + 1]
            some = total > 0
            safe = jnp.where(some, total, 1.0)
            out = acc[j, :HD] * jnp.where(some, 1.0 / safe, 0.0)
            level = top[j] + jnp.log2(safe)
            if j < 2:
                own_ref[j] = out
                ownl_ref[j] = level
            else:
                send_ref[j - 2, :HD] = out.astype(BF16)
                hi = level.astype(BF16).astype(F32)
                mid = (level - hi).astype(BF16).astype(F32)
                row = lax.broadcasted_iota(jnp.int32, (OUTR - HD, ROWS), 0)
                tail = jnp.where(row == 0, hi, jnp.where(row == 1, mid, level - hi - mid))
                send_ref[j - 2, HD:] = tail.astype(BF16)


def arrange(k_ref, v_ref, q_ref, out_ref, qout_ref):
    for h in range(HEADS):
        qout_ref[h] = q_ref[:, h * ROWS : (h + 1) * ROWS]
    for h in range(HEADS):
        cols = slice(h * HD, (h + 1) * HD)
        both = jnp.concatenate([k_ref[:, cols], v_ref[:, cols]], axis=1)
        for z in range(NZ // 2):
            out_ref[h, z] = both


def merge(own_ref, ownl_ref, got_ref, out_ref):
    for j in range(2):
        tail = got_ref[j, HD:].astype(F32)
        theirs = tail[0:1] + tail[1:2] + tail[2:3]
        mine = ownl_ref[j]
        high = jnp.maximum(mine, theirs)
        a, b = jnp.exp2(mine - high), jnp.exp2(theirs - high)
        inv = 1.0 / (a + b)
        out = own_ref[j] * (a * inv) + got_ref[j, :HD].astype(F32) * (b * inv)
        for h in range(GROUP):
            out_ref[j * CH : (j + 1) * CH, h * HD : (h + 1) * HD] = (
                out[:, h * CH : (h + 1) * CH].T.astype(BF16)
            )


VMEM = pl.BlockSpec(memory_space=pltpu.VMEM)
SMEM = pl.BlockSpec(memory_space=pltpu.SMEM)
SOURCES = (((0, 0),), ((1, 3), (3, 1)), ((2, 2),))
STAGES = len(SOURCES)


def call(stage, order, pos, *arrays):
    sources = SOURCES[stage]
    blocks = 2 * NZ * len(sources)
    state = (jax.ShapeDtypeStruct((4, OUTR, ROWS), F32), jax.ShapeDtypeStruct((4, 1, ROWS), F32))
    scratch = [
        pltpu.VMEM((blocks * CH, HD), BF16),
        pltpu.VMEM((OUTR, (blocks + 1) * CH), BF16),
        pltpu.VMEM((GB * CH, ROWS), F32),
        pltpu.VMEM((GB * CH, ROWS), F32),
        pltpu.SMEM((blocks + 16,), jnp.int32),
        pltpu.SMEM((GB * (blocks + 16),), jnp.int32),
        pltpu.SMEM((GB * (blocks + 16),), jnp.int32),
    ]
    if stage == 0:
        outs = state + (jax.ShapeDtypeStruct((4, 2 * HD, ROWS), BF16),)
    elif stage < STAGES - 1:
        outs = state
    else:
        outs = (
            jax.ShapeDtypeStruct((2, HD, ROWS), F32),
            jax.ShapeDtypeStruct((2, 1, ROWS), F32),
            jax.ShapeDtypeStruct((2, OUTR, ROWS), BF16),
        )
        scratch += [pltpu.VMEM((4, OUTR, ROWS), F32), pltpu.VMEM((4, 1, ROWS), F32)]
    flops = blocks * 2 * 2 * 2 * HD * CH * ROWS
    return pl.pallas_call(
        functools.partial(attend, stage, sources),
        out_shape=outs,
        in_specs=[SMEM] * 2 + [VMEM] * len(arrays),
        out_specs=(VMEM,) * len(outs),
        scratch_shapes=scratch,
        cost_estimate=pl.CostEstimate(flops=2 * flops, bytes_accessed=blocks * CH * 512, transcendentals=blocks * 2 * CH * ROWS),
        compiler_params=pltpu.CompilerParams(vmem_limit_bytes=20 << 20),
        name=f"attend{stage}",
    )(order, pos, *arrays)


def shards(queries, keys, values, order):
    def around(s):
        return [(c * NX + i, c * NX + (i + (s if c else -s)) % NX) for c in range(2) for i in range(NX)]

    def along_z(z, c):
        return ((z % 4 * 2) + c) * 2 + z // 4

    beside = [(along_z(z, c), along_z((z + (1 if c else -1)) % NZ, c)) for z in range(NZ) for c in range(2)]

    kv, q = pl.pallas_call(
        arrange,
        out_shape=(
            jax.ShapeDtypeStruct((HEADS, NZ // 2, SLICE, 2 * HD), BF16),
            jax.ShapeDtypeStruct((HEADS, SLICE, ROWS), BF16),
        ),
        in_specs=[VMEM] * 3,
        out_specs=(VMEM,) * 2,
        name="arrange",
    )(keys, values, queries)
    kv = lax.all_to_all(
        kv.reshape(HEADS * NZ // 2, SLICE, 2 * HD), ("head", "zhi", "zmid"), split_axis=0, concat_axis=0, tiled=True
    ).reshape(HEADS, NZ // 2, SLICE, 2 * HD)
    kv0 = jnp.stack([kv, lax.ppermute(kv, ("zmid", "zlow", "core", "zhi"), beside)])
    q = lax.all_to_all(q, "head", split_axis=0, concat_axis=0, tiled=True).reshape(2 * CH, ROWS)
    kv1 = lax.ppermute(kv0, ("core", "x"), around(1))
    kv3 = lax.ppermute(kv0, ("core", "x"), around(-1))
    qo = lax.ppermute(q, "core", [(0, 1), (1, 0)])
    pos = jnp.stack(
        [lax.axis_index("x"), lax.axis_index("zhi") * 4 + lax.axis_index("zmid") * 2 + lax.axis_index("zlow"), lax.axis_index("core")]
    ).astype(jnp.int32)
    acc, top, qt = call(0, order, pos, kv0, q, qo)
    kv1, top = lax.optimization_barrier((kv1, top))
    kv2 = lax.ppermute(kv1, ("core", "x"), around(1))
    acc, top = call(1, order, pos, kv1, kv3, qt, acc, top)
    own, ownl, send = call(2, order, pos, kv2, qt, acc, top)
    got = lax.ppermute(send, "core", [(0, 1), (1, 0)])
    out = pl.pallas_call(
        merge,
        out_shape=jax.ShapeDtypeStruct((2 * CH, ROWS), BF16),
        in_specs=[VMEM] * 3,
        out_specs=VMEM,
        compiler_params=pltpu.CompilerParams(vmem_limit_bytes=20 << 20),
        name="merge",
    )(own, ownl, got)
    return lax.all_to_all(out, "head", split_axis=0, concat_axis=1, tiled=True)


def solution(mesh):
    split = Mesh(mesh.devices.reshape(HEADS, 2, 2, 2, NX, 2), ("head", "zmid", "zlow", "core", "x", "zhi"))
    rows = P(("x", "zhi", "zmid", "zlow", "core", "head"), None)
    return jax.shard_map(
        shards, mesh=split, in_specs=(rows, rows, rows, P()), out_specs=rows, check_vma=False
    )
```

```python
import functools
import math

import jax
import jax.numpy as jnp
from jax import lax
from jax.experimental import pallas as pl
from jax.experimental.pallas import tpu as pltpu
from jax.sharding import Mesh, PartitionSpec as P

HEADS = 8
GROUP = 6
HD = 128
CH = 128
ROWS = GROUP * CH
NX, NZ = 4, 8
SLICE = CH // 4
C = math.log2(math.e) / math.sqrt(HD)
LOW = -1e30
MASKED = -3e38
GB = 4
WIDTH = 768
BEHIND = 0
OUTR = HD + 16
F32, BF16 = jnp.float32, jnp.bfloat16


def spread_queries(q_ref, qt, j, w):
    for h in range(GROUP):
        t = q_ref[w * CH : (w + 1) * CH, h * HD : (h + 1) * HD].T.astype(F32) * C
        hi = t.astype(BF16)
        qt[j, :HD, h * CH : (h + 1) * CH] = hi
        qt[j, HD:, h * CH : (h + 1) * CH] = (t - hi.astype(F32)).astype(BF16)


def fill(piece, at, kbuf, vt):
    for i in range(2 * NZ):
        w = i % 2
        to = (at + i) * CH
        block = piece[i // 8, 4 * w : 4 * w + 4, i // 2 % 4].reshape(CH, 2 * HD)
        kbuf[to : to + CH, :] = block[:, :HD]
        vt[:HD, to : to + CH] = block[:, HD:].T


def attend(stage, sources, *refs):
    first, last = stage == 0, stage == STAGES - 1
    order, pos = refs[:2]
    refs = refs[2:]
    pieces, refs = refs[: len(sources)], refs[len(sources) :]
    if first:
        q_ref, qo_ref, acc, top, qt = refs[:5]
        refs = refs[5:]
    elif not last:
        qt, acc_in, top_in, acc, top = refs[:5]
        refs = refs[5:]
    else:
        qt, acc_in, top_in, own_ref, ownl_ref, send_ref = refs[:6]
        refs = refs[6:]
        acc, top = acc_in, top_in
        refs, (acc, top) = refs[:-2], refs[-2:]
    kbuf, vt, sa, sb, tabj, tabk, tabv = refs
    x, z, core = pos[0], pos[1], pos[2]

    def stored(xv, zv, cv, w):
        return ((xv * NZ + zv) * 2 + cv) * 2 + w

    blocks = 2 * NZ * len(sources)
    dummy = blocks

    t = jnp.int32(0)
    for j in range(4):
        cv = core if j < 2 else 1 - core
        mine = order[stored(x, z, cv, j % 2)]
        n = t * GB
        start = n
        slot = 0
        for shifts in sources:
            xv = (x + jnp.where(core == 0, *shifts)) % NX

            for i in range(2 * NZ):
                zv = i // 2 % 4 * 2 + (z + i // 8) % 2
                tabk[n] = i + slot
                tabv[n] = i + slot
                n = n + (order[stored(xv, zv, core, i % 2)] < mine).astype(jnp.int32)
            slot += 2 * NZ
        steps = (n - start + GB - 1) // GB
        keep = tabk[jnp.maximum(n - 1, 0)]
        for g in range(GB - 1):
            tabk[n + g] = keep
            tabv[n + g] = dummy

        def mark(i, c, j=j):
            tabj[i] = j
            return c

        lax.fori_loop(t, t + steps, mark, 0)
        t = t + steps
    for e in range(3):
        back = jnp.maximum(t - 1, 0)
        tabj[t + e] = jnp.where(t > 0, tabj[back], 0)
        for g in range(GB):
            tabk[(t + e) * GB + g] = jnp.where(t > 0, tabk[back * GB + g], 0)
            tabv[(t + e) * GB + g] = dummy

    for at, piece in enumerate(pieces):
        fill(piece, at * 2 * NZ, kbuf, vt)
    vt[HD:, : blocks * CH] = jnp.ones((OUTR - HD, blocks * CH), BF16)
    vt[:, blocks * CH :] = jnp.zeros((OUTR, CH), BF16)

    def scores(i, out):
        k = jnp.concatenate(
            [kbuf[pl.ds(pl.multiple_of(tabk[i * GB + g] * CH, CH), CH), :] for g in range(GB)], axis=0
        )
        out[...] = jnp.dot(jnp.concatenate([k, k], axis=1), qt[tabj[i]], preferred_element_type=F32)

    def gather(i, s_ref):
        j = tabj[i]
        v = jnp.concatenate([vt[:, pl.ds(pl.multiple_of(tabv[i * GB + g] * CH, CH), CH)] for g in range(GB)], axis=1)
        s = s_ref[...]
        old = top[j]
        new = jnp.maximum(old, jnp.max(s, axis=0, keepdims=True))
        p = jnp.exp2(s - new).astype(BF16)
        acc[j] = acc[j] * jnp.exp2(old - new) + jnp.dot(v, p, preferred_element_type=F32)
        top[j] = new

    if first:
        for j in range(4):
            spread_queries(q_ref if j < 2 else qo_ref, qt, j, j % 2)
        below = lax.broadcasted_iota(jnp.int32, (CH, CH), 0) <= lax.broadcasted_iota(jnp.int32, (CH, CH), 1)
        below = jnp.concatenate([below] * GROUP, axis=1)
        for j in range(2):
            r = pl.multiple_of((z // 2 * 2 + j) * CH, CH)
            k = kbuf[pl.ds(r, CH), :]
            s = jnp.dot(jnp.concatenate([k, k], axis=1), qt[j], preferred_element_type=F32)
            s = jnp.where(below, s, MASKED)
            high = jnp.max(s, axis=0, keepdims=True)
            p = jnp.exp2(s - high).astype(BF16)
            acc[j] = jnp.dot(vt[:, pl.ds(r, CH)], p, preferred_element_type=F32)
            top[j] = high
        for j in range(2, 4):
            acc[j] = jnp.zeros((OUTR, ROWS), F32)
            top[j] = jnp.full((1, ROWS), LOW, F32)
    else:
        acc[...] = acc_in[...]
        top[...] = top_in[...]

    scores(0, sa)

    def both(i, s_ref, n_ref):
        j, jn = tabj[i], tabj[i + 1]
        k = jnp.concatenate(
            [kbuf[pl.ds(pl.multiple_of(tabk[(i + 1) * GB + g] * CH, CH), CH), :] for g in range(GB)], axis=0
        )
        k = jnp.concatenate([k, k], axis=1)
        v = jnp.concatenate([vt[:, pl.ds(pl.multiple_of(tabv[i * GB + g] * CH, CH), CH)] for g in range(GB)], axis=1)

        def add(cs, old, new, p):
            acc[j, :, cs] = acc[j, :, cs] * jnp.exp2(old - new) + jnp.dot(v, p, preferred_element_type=F32)
            top[j, :, cs] = new

        waiting = []
        for c in range(ROWS // WIDTH):
            cs = slice(c * WIDTH, (c + 1) * WIDTH)
            n_ref[:, cs] = jnp.dot(k, qt[jn, :, cs], preferred_element_type=F32)
            s = s_ref[:, cs]
            old = top[j, :, cs]
            new = jnp.maximum(old, jnp.max(s, axis=0, keepdims=True))
            waiting.append((cs, old, new, jnp.exp2(s - new).astype(BF16)))
            if len(waiting) > BEHIND:
                add(*waiting.pop(0))
        for w in waiting:
            add(*w)

    def pair(i, c):
        both(2 * i, sa, sb)
        both(2 * i + 1, sb, sa)
        return c

    pairs = (t + 1) // 2

    def several(i, c):
        for e in range(4):
            pair(4 * i + e, c)
        return c

    many = pairs // 4
    lax.fori_loop(0, many, several, 0)
    lax.fori_loop(many * 4, pairs, pair, 0)

    if last:
        for j in range(4):
            total = acc[j, HD : HD + 1]
            some = total > 0
            safe = jnp.where(some, total, 1.0)
            out = acc[j, :HD] * jnp.where(some, 1.0 / safe, 0.0)
            level = top[j] + jnp.log2(safe)
            if j < 2:
                own_ref[j] = out
                ownl_ref[j] = level
            else:
                send_ref[j - 2, :HD] = out.astype(BF16)
                hi = level.astype(BF16).astype(F32)
                mid = (level - hi).astype(BF16).astype(F32)
                row = lax.broadcasted_iota(jnp.int32, (OUTR - HD, ROWS), 0)
                tail = jnp.where(row == 0, hi, jnp.where(row == 1, mid, level - hi - mid))
                send_ref[j - 2, HD:] = tail.astype(BF16)


def arrange(k_ref, v_ref, q_ref, out_ref, qout_ref):
    for h in range(HEADS):
        qout_ref[h] = q_ref[:, h * ROWS : (h + 1) * ROWS]
    for h in range(HEADS):
        cols = slice(h * HD, (h + 1) * HD)
        both = jnp.concatenate([k_ref[:, cols], v_ref[:, cols]], axis=1)
        for z in range(NZ // 2):
            out_ref[h, z] = both


def merge(own_ref, ownl_ref, got_ref, out_ref):
    for j in range(2):
        tail = got_ref[j, HD:].astype(F32)
        theirs = tail[0:1] + tail[1:2] + tail[2:3]
        mine = ownl_ref[j]
        high = jnp.maximum(mine, theirs)
        a, b = jnp.exp2(mine - high), jnp.exp2(theirs - high)
        inv = 1.0 / (a + b)
        out = own_ref[j] * (a * inv) + got_ref[j, :HD].astype(F32) * (b * inv)
        for h in range(GROUP):
            out_ref[j * CH : (j + 1) * CH, h * HD : (h + 1) * HD] = (
                out[:, h * CH : (h + 1) * CH].T.astype(BF16)
            )


VMEM = pl.BlockSpec(memory_space=pltpu.VMEM)
SMEM = pl.BlockSpec(memory_space=pltpu.SMEM)
SOURCES = (((0, 0),), ((1, 3), (3, 1)), ((2, 2),))
STAGES = len(SOURCES)


def call(stage, order, pos, *arrays):
    sources = SOURCES[stage]
    blocks = 2 * NZ * len(sources)
    state = (jax.ShapeDtypeStruct((4, OUTR, ROWS), F32), jax.ShapeDtypeStruct((4, 1, ROWS), F32))
    scratch = [
        pltpu.VMEM((blocks * CH, HD), BF16),
        pltpu.VMEM((OUTR, (blocks + 1) * CH), BF16),
        pltpu.VMEM((GB * CH, ROWS), F32),
        pltpu.VMEM((GB * CH, ROWS), F32),
        pltpu.SMEM((blocks + 16,), jnp.int32),
        pltpu.SMEM((GB * (blocks + 16),), jnp.int32),
        pltpu.SMEM((GB * (blocks + 16),), jnp.int32),
    ]
    if stage == 0:
        outs = state + (jax.ShapeDtypeStruct((4, 2 * HD, ROWS), BF16),)
    elif stage < STAGES - 1:
        outs = state
    else:
        outs = (
            jax.ShapeDtypeStruct((2, HD, ROWS), F32),
            jax.ShapeDtypeStruct((2, 1, ROWS), F32),
            jax.ShapeDtypeStruct((2, OUTR, ROWS), BF16),
        )
        scratch += [pltpu.VMEM((4, OUTR, ROWS), F32), pltpu.VMEM((4, 1, ROWS), F32)]
    flops = blocks * 2 * 2 * 2 * HD * CH * ROWS
    return pl.pallas_call(
        functools.partial(attend, stage, sources),
        out_shape=outs,
        in_specs=[SMEM] * 2 + [VMEM] * len(arrays),
        out_specs=(VMEM,) * len(outs),
        scratch_shapes=scratch,
        cost_estimate=pl.CostEstimate(flops=2 * flops, bytes_accessed=blocks * CH * 512, transcendentals=blocks * 2 * CH * ROWS),
        compiler_params=pltpu.CompilerParams(vmem_limit_bytes=20 << 20),
        name=f"attend{stage}",
    )(order, pos, *arrays)


def shards(queries, keys, values, order):
    def around(s):
        return [(c * NX + i, c * NX + (i + (s if c else -s)) % NX) for c in range(2) for i in range(NX)]

    def along_z(z, c):
        return ((z % 4 * 2) + c) * 2 + z // 4

    beside = [(along_z(z, c), along_z((z + (1 if c else -1)) % NZ, c)) for z in range(NZ) for c in range(2)]

    kv, q = pl.pallas_call(
        arrange,
        out_shape=(
            jax.ShapeDtypeStruct((HEADS, NZ // 2, SLICE, 2 * HD), BF16),
            jax.ShapeDtypeStruct((HEADS, SLICE, ROWS), BF16),
        ),
        in_specs=[VMEM] * 3,
        out_specs=(VMEM,) * 2,
        name="arrange",
    )(keys, values, queries)
    kv = lax.all_to_all(
        kv.reshape(HEADS * NZ // 2, SLICE, 2 * HD), ("head", "zhi", "zmid"), split_axis=0, concat_axis=0, tiled=True
    ).reshape(HEADS, NZ // 2, SLICE, 2 * HD)
    kvz = lax.ppermute(kv, ("zmid", "zlow", "core", "zhi"), beside)
    kv0 = jnp.stack([kv, kvz])
    q = lax.all_to_all(q, "head", split_axis=0, concat_axis=0, tiled=True).reshape(2 * CH, ROWS)
    near = [lax.ppermute(part, ("core", "x"), around(1)) for part in (kv, kvz)]
    near[0], near[1], q = lax.optimization_barrier((near[0], near[1], q))
    kv1 = jnp.stack(near)
    kv3 = lax.ppermute(kv0, ("core", "x"), around(-1))
    qo = lax.ppermute(q, "core", [(0, 1), (1, 0)])
    pos = jnp.stack(
        [lax.axis_index("x"), lax.axis_index("zhi") * 4 + lax.axis_index("zmid") * 2 + lax.axis_index("zlow"), lax.axis_index("core")]
    ).astype(jnp.int32)
    acc, top, qt = call(0, order, pos, kv0, q, qo)
    kv1, top = lax.optimization_barrier((kv1, top))
    kv2 = lax.ppermute(kv1, ("core", "x"), around(1))
    acc, top = call(1, order, pos, kv1, kv3, qt, acc, top)
    own, ownl, send = call(2, order, pos, kv2, qt, acc, top)
    got = lax.ppermute(send, "core", [(0, 1), (1, 0)])
    out = pl.pallas_call(
        merge,
        out_shape=jax.ShapeDtypeStruct((2 * CH, ROWS), BF16),
        in_specs=[VMEM] * 3,
        out_specs=VMEM,
        compiler_params=pltpu.CompilerParams(vmem_limit_bytes=20 << 20),
        name="merge",
    )(own, ownl, got)
    return lax.all_to_all(out, "head", split_axis=0, concat_axis=1, tiled=True)


def solution(mesh):
    split = Mesh(mesh.devices.reshape(HEADS, 2, 2, 2, NX, 2), ("head", "zmid", "zlow", "core", "x", "zhi"))
    rows = P(("x", "zhi", "zmid", "zlow", "core", "head"), None)
    return jax.shard_map(
        shards, mesh=split, in_specs=(rows, rows, rows, P()), out_specs=rows, check_vma=False
    )
```

```python
import functools
import math

import jax
import jax.numpy as jnp
from jax import lax
from jax.experimental import pallas as pl
from jax.experimental.pallas import tpu as pltpu
from jax.sharding import Mesh, PartitionSpec as P

HEADS = 8
GROUP = 6
HD = 128
CH = 128
ROWS = GROUP * CH
NX, NZ = 4, 8
SLICE = CH // 4
C = math.log2(math.e) / math.sqrt(HD)
LOW = -1e30
MASKED = -3e38
GB = 4
WIDTH = 768
BEHIND = 0
OUTR = HD + 16
F32, BF16 = jnp.float32, jnp.bfloat16


def spread_queries(q_ref, qt, j, w):
    for h in range(GROUP):
        t = q_ref[w * CH : (w + 1) * CH, h * HD : (h + 1) * HD].T.astype(F32) * C
        hi = t.astype(BF16)
        qt[j, :HD, h * CH : (h + 1) * CH] = hi
        qt[j, HD:, h * CH : (h + 1) * CH] = (t - hi.astype(F32)).astype(BF16)


def fill(piece, at, kbuf, vt):
    for i in range(2 * NZ):
        w = i % 2
        to = (at + i) * CH
        block = piece[i // 8, 4 * w : 4 * w + 4, i // 2 % 4].reshape(CH, 2 * HD)
        kbuf[to : to + CH, :] = block[:, :HD]
        vt[:HD, to : to + CH] = block[:, HD:].T


def attend(stage, sources, *refs):
    first, last = stage == 0, stage == STAGES - 1
    order, pos = refs[:2]
    refs = refs[2:]
    pieces, refs = refs[: len(sources)], refs[len(sources) :]
    if first:
        q_ref, qo_ref, acc, top, qt = refs[:5]
        refs = refs[5:]
    elif not last:
        qt, acc_in, top_in, acc, top = refs[:5]
        refs = refs[5:]
    else:
        qt, acc_in, top_in, own_ref, ownl_ref, send_ref = refs[:6]
        refs = refs[6:]
        acc, top = acc_in, top_in
        refs, (acc, top) = refs[:-2], refs[-2:]
    kbuf, vt, sa, sb, tabj, tabk, tabv = refs
    x, z, core = pos[0], pos[1], pos[2]

    def stored(xv, zv, cv, w):
        return ((xv * NZ + zv) * 2 + cv) * 2 + w

    blocks = 2 * NZ * len(sources)
    dummy = blocks

    t = jnp.int32(0)
    for j in range(4):
        cv = core if j < 2 else 1 - core
        mine = order[stored(x, z, cv, j % 2)]
        n = t * GB
        start = n
        slot = 0
        for shifts in sources:
            xv = (x + jnp.where(core == 0, *shifts)) % NX

            for i in range(2 * NZ):
                zv = i // 2 % 4 * 2 + (z + i // 8) % 2
                tabk[n] = i + slot
                tabv[n] = i + slot
                n = n + (order[stored(xv, zv, core, i % 2)] < mine).astype(jnp.int32)
            slot += 2 * NZ
        steps = (n - start + GB - 1) // GB
        keep = tabk[jnp.maximum(n - 1, 0)]
        for g in range(GB - 1):
            tabk[n + g] = keep
            tabv[n + g] = dummy

        def mark(i, c, j=j):
            tabj[i] = j
            return c

        lax.fori_loop(t, t + steps, mark, 0)
        t = t + steps
    for e in range(3):
        back = jnp.maximum(t - 1, 0)
        tabj[t + e] = jnp.where(t > 0, tabj[back], 0)
        for g in range(GB):
            tabk[(t + e) * GB + g] = jnp.where(t > 0, tabk[back * GB + g], 0)
            tabv[(t + e) * GB + g] = dummy

    for at, piece in enumerate(pieces):
        fill(piece, at * 2 * NZ, kbuf, vt)
    vt[HD:, : blocks * CH] = jnp.ones((OUTR - HD, blocks * CH), BF16)
    vt[:, blocks * CH :] = jnp.zeros((OUTR, CH), BF16)

    def scores(i, out):
        k = jnp.concatenate(
            [kbuf[pl.ds(pl.multiple_of(tabk[i * GB + g] * CH, CH), CH), :] for g in range(GB)], axis=0
        )
        out[...] = jnp.dot(jnp.concatenate([k, k], axis=1), qt[tabj[i]], preferred_element_type=F32)

    def gather(i, s_ref):
        j = tabj[i]
        v = jnp.concatenate([vt[:, pl.ds(pl.multiple_of(tabv[i * GB + g] * CH, CH), CH)] for g in range(GB)], axis=1)
        s = s_ref[...]
        old = top[j]
        new = jnp.maximum(old, jnp.max(s, axis=0, keepdims=True))
        p = jnp.exp2(s - new).astype(BF16)
        acc[j] = acc[j] * jnp.exp2(old - new) + jnp.dot(v, p, preferred_element_type=F32)
        top[j] = new

    if first:
        for j in range(4):
            spread_queries(q_ref if j < 2 else qo_ref, qt, j, j % 2)
        below = lax.broadcasted_iota(jnp.int32, (CH, CH), 0) <= lax.broadcasted_iota(jnp.int32, (CH, CH), 1)
        below = jnp.concatenate([below] * GROUP, axis=1)
        for j in range(2):
            r = pl.multiple_of((z // 2 * 2 + j) * CH, CH)
            k = kbuf[pl.ds(r, CH), :]
            s = jnp.dot(jnp.concatenate([k, k], axis=1), qt[j], preferred_element_type=F32)
            s = jnp.where(below, s, MASKED)
            high = jnp.max(s, axis=0, keepdims=True)
            p = jnp.exp2(s - high).astype(BF16)
            acc[j] = jnp.dot(vt[:, pl.ds(r, CH)], p, preferred_element_type=F32)
            top[j] = high
        for j in range(2, 4):
            acc[j] = jnp.zeros((OUTR, ROWS), F32)
            top[j] = jnp.full((1, ROWS), LOW, F32)
    else:
        acc[...] = acc_in[...]
        top[...] = top_in[...]

    scores(0, sa)

    def both(i, s_ref, n_ref):
        j, jn = tabj[i], tabj[i + 1]
        k = jnp.concatenate(
            [kbuf[pl.ds(pl.multiple_of(tabk[(i + 1) * GB + g] * CH, CH), CH), :] for g in range(GB)], axis=0
        )
        k = jnp.concatenate([k, k], axis=1)
        v = jnp.concatenate([vt[:, pl.ds(pl.multiple_of(tabv[i * GB + g] * CH, CH), CH)] for g in range(GB)], axis=1)

        def add(cs, old, new, p):
            acc[j, :, cs] = acc[j, :, cs] * jnp.exp2(old - new) + jnp.dot(v, p, preferred_element_type=F32)
            top[j, :, cs] = new

        waiting = []
        for c in range(ROWS // WIDTH):
            cs = slice(c * WIDTH, (c + 1) * WIDTH)
            n_ref[:, cs] = jnp.dot(k, qt[jn, :, cs], preferred_element_type=F32)
            s = s_ref[:, cs]
            old = top[j, :, cs]
            new = jnp.maximum(old, jnp.max(s, axis=0, keepdims=True))
            waiting.append((cs, old, new, jnp.exp2(s - new).astype(BF16)))
            if len(waiting) > BEHIND:
                add(*waiting.pop(0))
        for w in waiting:
            add(*w)

    def pair(i, c):
        both(2 * i, sa, sb)
        both(2 * i + 1, sb, sa)
        return c

    pairs = (t + 1) // 2

    def several(i, c):
        for e in range(4):
            pair(4 * i + e, c)
        return c

    many = pairs // 4
    lax.fori_loop(0, many, several, 0)
    lax.fori_loop(many * 4, pairs, pair, 0)

    if last:
        for j in range(4):
            total = acc[j, HD : HD + 1]
            some = total > 0
            safe = jnp.where(some, total, 1.0)
            out = acc[j, :HD] * jnp.where(some, 1.0 / safe, 0.0)
            level = top[j] + jnp.log2(safe)
            if j < 2:
                own_ref[j] = out
                ownl_ref[j] = level
            else:
                send_ref[j - 2, :HD] = out.astype(BF16)
                hi = level.astype(BF16).astype(F32)
                mid = (level - hi).astype(BF16).astype(F32)
                row = lax.broadcasted_iota(jnp.int32, (OUTR - HD, ROWS), 0)
                tail = jnp.where(row == 0, hi, jnp.where(row == 1, mid, level - hi - mid))
                send_ref[j - 2, HD:] = tail.astype(BF16)


def arrange(k_ref, v_ref, q_ref, out_ref, qout_ref):
    for h in range(HEADS):
        qout_ref[h] = q_ref[:, h * ROWS : (h + 1) * ROWS]
    for h in range(HEADS):
        cols = slice(h * HD, (h + 1) * HD)
        both = jnp.concatenate([k_ref[:, cols], v_ref[:, cols]], axis=1)
        for z in range(NZ // 2):
            out_ref[h, z] = both


def merge(own_ref, ownl_ref, got_ref, out_ref):
    for j in range(2):
        tail = got_ref[j, HD:].astype(F32)
        theirs = tail[0:1] + tail[1:2] + tail[2:3]
        mine = ownl_ref[j]
        high = jnp.maximum(mine, theirs)
        a, b = jnp.exp2(mine - high), jnp.exp2(theirs - high)
        inv = 1.0 / (a + b)
        out = own_ref[j] * (a * inv) + got_ref[j, :HD].astype(F32) * (b * inv)
        for h in range(GROUP):
            out_ref[j * CH : (j + 1) * CH, h * HD : (h + 1) * HD] = (
                out[:, h * CH : (h + 1) * CH].T.astype(BF16)
            )


VMEM = pl.BlockSpec(memory_space=pltpu.VMEM)
SMEM = pl.BlockSpec(memory_space=pltpu.SMEM)
SOURCES = (((0, 0),), ((1, 3), (3, 1)), ((2, 2),))
STAGES = len(SOURCES)


def call(stage, order, pos, *arrays):
    sources = SOURCES[stage]
    blocks = 2 * NZ * len(sources)
    state = (jax.ShapeDtypeStruct((4, OUTR, ROWS), F32), jax.ShapeDtypeStruct((4, 1, ROWS), F32))
    scratch = [
        pltpu.VMEM((blocks * CH, HD), BF16),
        pltpu.VMEM((OUTR, (blocks + 1) * CH), BF16),
        pltpu.VMEM((GB * CH, ROWS), F32),
        pltpu.VMEM((GB * CH, ROWS), F32),
        pltpu.SMEM((blocks + 16,), jnp.int32),
        pltpu.SMEM((GB * (blocks + 16),), jnp.int32),
        pltpu.SMEM((GB * (blocks + 16),), jnp.int32),
    ]
    if stage == 0:
        outs = state + (jax.ShapeDtypeStruct((4, 2 * HD, ROWS), BF16),)
    elif stage < STAGES - 1:
        outs = state
    else:
        outs = (
            jax.ShapeDtypeStruct((2, HD, ROWS), F32),
            jax.ShapeDtypeStruct((2, 1, ROWS), F32),
            jax.ShapeDtypeStruct((2, OUTR, ROWS), BF16),
        )
        scratch += [pltpu.VMEM((4, OUTR, ROWS), F32), pltpu.VMEM((4, 1, ROWS), F32)]
    flops = blocks * 2 * 2 * 2 * HD * CH * ROWS
    return pl.pallas_call(
        functools.partial(attend, stage, sources),
        out_shape=outs,
        in_specs=[SMEM] * 2 + [VMEM] * len(arrays),
        out_specs=(VMEM,) * len(outs),
        scratch_shapes=scratch,
        cost_estimate=pl.CostEstimate(flops=2 * flops, bytes_accessed=blocks * CH * 512, transcendentals=blocks * 2 * CH * ROWS),
        compiler_params=pltpu.CompilerParams(vmem_limit_bytes=20 << 20),
        name=f"attend{stage}",
    )(order, pos, *arrays)


def shards(queries, keys, values, order):
    def around(s):
        return [(c * NX + i, c * NX + (i + (s if c else -s)) % NX) for c in range(2) for i in range(NX)]

    def along_z(z, c):
        return ((z % 4 * 2) + c) * 2 + z // 4

    beside = [(along_z(z, c), along_z((z + (1 if c else -1)) % NZ, c)) for z in range(NZ) for c in range(2)]

    kv, q = pl.pallas_call(
        arrange,
        out_shape=(
            jax.ShapeDtypeStruct((HEADS, NZ // 2, SLICE, 2 * HD), BF16),
            jax.ShapeDtypeStruct((HEADS, SLICE, ROWS), BF16),
        ),
        in_specs=[VMEM] * 3,
        out_specs=(VMEM,) * 2,
        name="arrange",
    )(keys, values, queries)
    kv = lax.all_to_all(
        kv.reshape(HEADS * NZ // 2, SLICE, 2 * HD), ("head", "zhi", "zmid"), split_axis=0, concat_axis=0, tiled=True
    ).reshape(HEADS, NZ // 2, SLICE, 2 * HD)
    kv0 = jnp.stack([kv, lax.ppermute(kv, ("zmid", "zlow", "core", "zhi"), beside)])
    q = lax.all_to_all(q, "head", split_axis=0, concat_axis=0, tiled=True).reshape(2 * CH, ROWS)
    kv1 = lax.ppermute(kv0, ("core", "x"), around(1))
    late, q = lax.optimization_barrier((kv0, q))
    kv3 = lax.ppermute(late, ("core", "x"), around(-1))
    qo = lax.ppermute(q, "core", [(0, 1), (1, 0)])
    pos = jnp.stack(
        [lax.axis_index("x"), lax.axis_index("zhi") * 4 + lax.axis_index("zmid") * 2 + lax.axis_index("zlow"), lax.axis_index("core")]
    ).astype(jnp.int32)
    acc, top, qt = call(0, order, pos, kv0, q, qo)
    kv1, top = lax.optimization_barrier((kv1, top))
    kv2 = lax.ppermute(kv1, ("core", "x"), around(1))
    acc, top = call(1, order, pos, kv1, kv3, qt, acc, top)
    own, ownl, send = call(2, order, pos, kv2, qt, acc, top)
    got = lax.ppermute(send, "core", [(0, 1), (1, 0)])
    out = pl.pallas_call(
        merge,
        out_shape=jax.ShapeDtypeStruct((2 * CH, ROWS), BF16),
        in_specs=[VMEM] * 3,
        out_specs=VMEM,
        compiler_params=pltpu.CompilerParams(vmem_limit_bytes=20 << 20),
        name="merge",
    )(own, ownl, got)
    return lax.all_to_all(out, "head", split_axis=0, concat_axis=1, tiled=True)


def solution(mesh):
    split = Mesh(mesh.devices.reshape(HEADS, 2, 2, 2, NX, 2), ("head", "zmid", "zlow", "core", "x", "zhi"))
    rows = P(("x", "zhi", "zmid", "zlow", "core", "head"), None)
    return jax.shard_map(
        shards, mesh=split, in_specs=(rows, rows, rows, P()), out_specs=rows, check_vma=False
    )
```

```python
import functools
import math

import jax
import jax.numpy as jnp
from jax import lax
from jax.experimental import pallas as pl
from jax.experimental.pallas import tpu as pltpu
from jax.sharding import Mesh, PartitionSpec as P

HEADS = 8
GROUP = 6
HD = 128
CH = 128
ROWS = GROUP * CH
NX, NZ = 4, 8
SLICE = CH // 4
C = math.log2(math.e) / math.sqrt(HD)
LOW = -1e30
MASKED = -3e38
GB = 4
WIDTH = 768
BEHIND = 0
OUTR = HD + 16
F32, BF16 = jnp.float32, jnp.bfloat16


def spread_queries(q_ref, qt, j, w):
    for h in range(GROUP):
        t = q_ref[w * CH : (w + 1) * CH, h * HD : (h + 1) * HD].T.astype(F32) * C
        hi = t.astype(BF16)
        qt[j, :HD, h * CH : (h + 1) * CH] = hi
        qt[j, HD:, h * CH : (h + 1) * CH] = (t - hi.astype(F32)).astype(BF16)


def fill(sets, at, kbuf, vt):
    for i in range(2 * NZ):
        w = i % 2
        to = (at + i) * CH
        block = sets[i // 8][4 * w : 4 * w + 4, i // 2 % 4].reshape(CH, 2 * HD)
        kbuf[to : to + CH, :] = block[:, :HD]
        vt[:HD, to : to + CH] = block[:, HD:].T


def attend(stage, sources, *refs):
    first, last = stage == 0, stage == STAGES - 1
    order, pos = refs[:2]
    refs = refs[2:]
    if last:
        pieces, refs = [refs[:2]], refs[2:]
    else:
        pieces = [(ref.at[0], ref.at[1]) for ref in refs[: len(sources)]]
        refs = refs[len(sources) :]
    if first:
        q_ref, qo_ref, acc, top, qt = refs[:5]
        refs = refs[5:]
    elif not last:
        qt, acc_in, top_in, acc, top = refs[:5]
        refs = refs[5:]
    else:
        qt, acc_in, top_in, own_ref, ownl_ref, send_ref = refs[:6]
        refs = refs[6:]
        acc, top = acc_in, top_in
        refs, (acc, top) = refs[:-2], refs[-2:]
    kbuf, vt, sa, sb, tabj, tabk, tabv = refs
    x, z, core = pos[0], pos[1], pos[2]

    def stored(xv, zv, cv, w):
        return ((xv * NZ + zv) * 2 + cv) * 2 + w

    blocks = 2 * NZ * len(sources)
    dummy = blocks

    t = jnp.int32(0)
    for j in range(4):
        cv = core if j < 2 else 1 - core
        mine = order[stored(x, z, cv, j % 2)]
        n = t * GB
        start = n
        slot = 0
        for shifts in sources:
            xv = (x + jnp.where(core == 0, *shifts)) % NX

            for i in range(2 * NZ):
                zv = i // 2 % 4 * 2 + (z + i // 8) % 2
                tabk[n] = i + slot
                tabv[n] = i + slot
                n = n + (order[stored(xv, zv, core, i % 2)] < mine).astype(jnp.int32)
            slot += 2 * NZ
        steps = (n - start + GB - 1) // GB
        keep = tabk[jnp.maximum(n - 1, 0)]
        for g in range(GB - 1):
            tabk[n + g] = keep
            tabv[n + g] = dummy

        def mark(i, c, j=j):
            tabj[i] = j
            return c

        lax.fori_loop(t, t + steps, mark, 0)
        t = t + steps
    for e in range(3):
        back = jnp.maximum(t - 1, 0)
        tabj[t + e] = jnp.where(t > 0, tabj[back], 0)
        for g in range(GB):
            tabk[(t + e) * GB + g] = jnp.where(t > 0, tabk[back * GB + g], 0)
            tabv[(t + e) * GB + g] = dummy

    for at, piece in enumerate(pieces):
        fill(piece, at * 2 * NZ, kbuf, vt)
    vt[HD:, : blocks * CH] = jnp.ones((OUTR - HD, blocks * CH), BF16)
    vt[:, blocks * CH :] = jnp.zeros((OUTR, CH), BF16)

    def scores(i, out):
        k = jnp.concatenate(
            [kbuf[pl.ds(pl.multiple_of(tabk[i * GB + g] * CH, CH), CH), :] for g in range(GB)], axis=0
        )
        out[...] = jnp.dot(jnp.concatenate([k, k], axis=1), qt[tabj[i]], preferred_element_type=F32)

    def gather(i, s_ref):
        j = tabj[i]
        v = jnp.concatenate([vt[:, pl.ds(pl.multiple_of(tabv[i * GB + g] * CH, CH), CH)] for g in range(GB)], axis=1)
        s = s_ref[...]
        old = top[j]
        new = jnp.maximum(old, jnp.max(s, axis=0, keepdims=True))
        p = jnp.exp2(s - new).astype(BF16)
        acc[j] = acc[j] * jnp.exp2(old - new) + jnp.dot(v, p, preferred_element_type=F32)
        top[j] = new

    if first:
        for j in range(4):
            spread_queries(q_ref if j < 2 else qo_ref, qt, j, j % 2)
        below = lax.broadcasted_iota(jnp.int32, (CH, CH), 0) <= lax.broadcasted_iota(jnp.int32, (CH, CH), 1)
        below = jnp.concatenate([below] * GROUP, axis=1)
        for j in range(2):
            r = pl.multiple_of((z // 2 * 2 + j) * CH, CH)
            k = kbuf[pl.ds(r, CH), :]
            s = jnp.dot(jnp.concatenate([k, k], axis=1), qt[j], preferred_element_type=F32)
            s = jnp.where(below, s, MASKED)
            high = jnp.max(s, axis=0, keepdims=True)
            p = jnp.exp2(s - high).astype(BF16)
            acc[j] = jnp.dot(vt[:, pl.ds(r, CH)], p, preferred_element_type=F32)
            top[j] = high
        for j in range(2, 4):
            acc[j] = jnp.zeros((OUTR, ROWS), F32)
            top[j] = jnp.full((1, ROWS), LOW, F32)
    else:
        acc[...] = acc_in[...]
        top[...] = top_in[...]

    scores(0, sa)

    def both(i, s_ref, n_ref):
        j, jn = tabj[i], tabj[i + 1]
        k = jnp.concatenate(
            [kbuf[pl.ds(pl.multiple_of(tabk[(i + 1) * GB + g] * CH, CH), CH), :] for g in range(GB)], axis=0
        )
        k = jnp.concatenate([k, k], axis=1)
        v = jnp.concatenate([vt[:, pl.ds(pl.multiple_of(tabv[i * GB + g] * CH, CH), CH)] for g in range(GB)], axis=1)

        def add(cs, old, new, p):
            acc[j, :, cs] = acc[j, :, cs] * jnp.exp2(old - new) + jnp.dot(v, p, preferred_element_type=F32)
            top[j, :, cs] = new

        waiting = []
        for c in range(ROWS // WIDTH):
            cs = slice(c * WIDTH, (c + 1) * WIDTH)
            n_ref[:, cs] = jnp.dot(k, qt[jn, :, cs], preferred_element_type=F32)
            s = s_ref[:, cs]
            old = top[j, :, cs]
            new = jnp.maximum(old, jnp.max(s, axis=0, keepdims=True))
            waiting.append((cs, old, new, jnp.exp2(s - new).astype(BF16)))
            if len(waiting) > BEHIND:
                add(*waiting.pop(0))
        for w in waiting:
            add(*w)

    def pair(i, c):
        both(2 * i, sa, sb)
        both(2 * i + 1, sb, sa)
        return c

    pairs = (t + 1) // 2

    def several(i, c):
        for e in range(4):
            pair(4 * i + e, c)
        return c

    many = pairs // 4
    lax.fori_loop(0, many, several, 0)
    lax.fori_loop(many * 4, pairs, pair, 0)

    if last:
        for j in range(4):
            total = acc[j, HD : HD + 1]
            some = total > 0
            safe = jnp.where(some, total, 1.0)
            out = acc[j, :HD] * jnp.where(some, 1.0 / safe, 0.0)
            level = top[j] + jnp.log2(safe)
            if j < 2:
                own_ref[j] = out
                ownl_ref[j] = level
            else:
                send_ref[j - 2, :HD] = out.astype(BF16)
                hi = level.astype(BF16).astype(F32)
                mid = (level - hi).astype(BF16).astype(F32)
                row = lax.broadcasted_iota(jnp.int32, (OUTR - HD, ROWS), 0)
                tail = jnp.where(row == 0, hi, jnp.where(row == 1, mid, level - hi - mid))
                send_ref[j - 2, HD:] = tail.astype(BF16)


def arrange(k_ref, v_ref, q_ref, out_ref, qout_ref):
    for h in range(HEADS):
        qout_ref[h] = q_ref[:, h * ROWS : (h + 1) * ROWS]
    for h in range(HEADS):
        cols = slice(h * HD, (h + 1) * HD)
        both = jnp.concatenate([k_ref[:, cols], v_ref[:, cols]], axis=1)
        for z in range(NZ // 2):
            out_ref[h, z] = both


def merge(own_ref, ownl_ref, got_ref, out_ref):
    for j in range(2):
        tail = got_ref[j, HD:].astype(F32)
        theirs = tail[0:1] + tail[1:2] + tail[2:3]
        mine = ownl_ref[j]
        high = jnp.maximum(mine, theirs)
        a, b = jnp.exp2(mine - high), jnp.exp2(theirs - high)
        inv = 1.0 / (a + b)
        out = own_ref[j] * (a * inv) + got_ref[j, :HD].astype(F32) * (b * inv)
        for h in range(GROUP):
            out_ref[j * CH : (j + 1) * CH, h * HD : (h + 1) * HD] = (
                out[:, h * CH : (h + 1) * CH].T.astype(BF16)
            )


VMEM = pl.BlockSpec(memory_space=pltpu.VMEM)
SMEM = pl.BlockSpec(memory_space=pltpu.SMEM)
SOURCES = (((0, 0),), ((1, 3), (3, 1)), ((2, 2),))
STAGES = len(SOURCES)


def call(stage, order, pos, *arrays):
    sources = SOURCES[stage]
    blocks = 2 * NZ * len(sources)
    state = (jax.ShapeDtypeStruct((4, OUTR, ROWS), F32), jax.ShapeDtypeStruct((4, 1, ROWS), F32))
    scratch = [
        pltpu.VMEM((blocks * CH, HD), BF16),
        pltpu.VMEM((OUTR, (blocks + 1) * CH), BF16),
        pltpu.VMEM((GB * CH, ROWS), F32),
        pltpu.VMEM((GB * CH, ROWS), F32),
        pltpu.SMEM((blocks + 16,), jnp.int32),
        pltpu.SMEM((GB * (blocks + 16),), jnp.int32),
        pltpu.SMEM((GB * (blocks + 16),), jnp.int32),
    ]
    if stage == 0:
        outs = state + (jax.ShapeDtypeStruct((4, 2 * HD, ROWS), BF16),)
    elif stage < STAGES - 1:
        outs = state
    else:
        outs = (
            jax.ShapeDtypeStruct((2, HD, ROWS), F32),
            jax.ShapeDtypeStruct((2, 1, ROWS), F32),
            jax.ShapeDtypeStruct((2, OUTR, ROWS), BF16),
        )
        scratch += [pltpu.VMEM((4, OUTR, ROWS), F32), pltpu.VMEM((4, 1, ROWS), F32)]
    flops = blocks * 2 * 2 * 2 * HD * CH * ROWS
    return pl.pallas_call(
        functools.partial(attend, stage, sources),
        out_shape=outs,
        in_specs=[SMEM] * 2 + [VMEM] * len(arrays),
        out_specs=(VMEM,) * len(outs),
        scratch_shapes=scratch,
        cost_estimate=pl.CostEstimate(flops=2 * flops, bytes_accessed=blocks * CH * 512, transcendentals=blocks * 2 * CH * ROWS),
        compiler_params=pltpu.CompilerParams(vmem_limit_bytes=20 << 20),
        name=f"attend{stage}",
    )(order, pos, *arrays)


def shards(queries, keys, values, order):
    def around(s):
        return [(c * NX + i, c * NX + (i + (s if c else -s)) % NX) for c in range(2) for i in range(NX)]

    def along_z(z, c):
        return ((z % 4 * 2) + c) * 2 + z // 4

    beside = [(along_z(z, c), along_z((z + (1 if c else -1)) % NZ, c)) for z in range(NZ) for c in range(2)]

    kv, q = pl.pallas_call(
        arrange,
        out_shape=(
            jax.ShapeDtypeStruct((HEADS, NZ // 2, SLICE, 2 * HD), BF16),
            jax.ShapeDtypeStruct((HEADS, SLICE, ROWS), BF16),
        ),
        in_specs=[VMEM] * 3,
        out_specs=(VMEM,) * 2,
        name="arrange",
    )(keys, values, queries)
    kv = lax.all_to_all(
        kv.reshape(HEADS * NZ // 2, SLICE, 2 * HD), ("head", "zhi", "zmid"), split_axis=0, concat_axis=0, tiled=True
    ).reshape(HEADS, NZ // 2, SLICE, 2 * HD)
    kv0 = jnp.stack([kv, lax.ppermute(kv, ("zmid", "zlow", "core", "zhi"), beside)])
    q = lax.all_to_all(q, "head", split_axis=0, concat_axis=0, tiled=True).reshape(2 * CH, ROWS)
    kv1 = lax.ppermute(kv0, ("core", "x"), around(1))
    late, q = lax.optimization_barrier((kv0, q))
    kv3 = lax.ppermute(late, ("core", "x"), around(-1))
    qo = lax.ppermute(q, "core", [(0, 1), (1, 0)])
    pos = jnp.stack(
        [lax.axis_index("x"), lax.axis_index("zhi") * 4 + lax.axis_index("zmid") * 2 + lax.axis_index("zlow"), lax.axis_index("core")]
    ).astype(jnp.int32)
    acc, top, qt = call(0, order, pos, kv0, q, qo)
    kv1, top = lax.optimization_barrier((kv1, top))
    far = [lax.ppermute(kv1[i], ("core", "x"), around(1)) for i in range(2)]
    acc, top = call(1, order, pos, kv1, kv3, qt, acc, top)
    own, ownl, send = call(2, order, pos, *far, qt, acc, top)
    got = lax.ppermute(send, "core", [(0, 1), (1, 0)])
    out = pl.pallas_call(
        merge,
        out_shape=jax.ShapeDtypeStruct((2 * CH, ROWS), BF16),
        in_specs=[VMEM] * 3,
        out_specs=VMEM,
        compiler_params=pltpu.CompilerParams(vmem_limit_bytes=20 << 20),
        name="merge",
    )(own, ownl, got)
    return lax.all_to_all(out, "head", split_axis=0, concat_axis=1, tiled=True)


def solution(mesh):
    split = Mesh(mesh.devices.reshape(HEADS, 2, 2, 2, NX, 2), ("head", "zmid", "zlow", "core", "x", "zhi"))
    rows = P(("x", "zhi", "zmid", "zlow", "core", "head"), None)
    return jax.shard_map(
        shards, mesh=split, in_specs=(rows, rows, rows, P()), out_specs=rows, check_vma=False
    )
```
